512 devices in a mesh: blk: 32 (over z, y_lo), off: 16 (over x, y_hi, core).
Axes of the slice: x: 4, y: 8 (y_hi: 2, y_lo: 4; y = y_hi * 4 + y_lo), z: 8, core: 2. Of those that a mesh axis runs over, the one named last changes fastest.
Arguments:
- orbitals: bfloat16 [32, 48, 2304], P('blk'), may hold values from -1.5 to 1.5
Outputs:
- exchange: float32 [32, 48, 2304], P('blk', 'off')
The draws below stay inside these ranges and needn't reach their ends.
All inputs are finite; a program needn't handle non-finite values.
Results may differ from the reference program's by a relative error of at most 0.00055.
Values may be sent and summed in bfloat16 or wider, within the bound.
A program may use at most 64 MiB of HBM per device.

```python
import math
import jax
import jax.numpy as jnp
from jax import lax

NG = 48
BANDS = 32


def steps_of(rng, shape, split, smallest, top_value):
    gain = 1.0
    for dim, parts in split:
        draws = jax.random.uniform(jax.random.fold_in(jax.random.fold_in(rng, 6), dim), (parts,), jnp.float32, smallest / len(split), top_value / len(split))
        gain = gain * jnp.repeat(jnp.exp(draws), shape[dim] // parts).reshape((-1,) + (1,) * (len(shape) - 1 - dim))
    return gain


def gaussian(own_key, dims, scale, bound, split=(), held_as=jnp.bfloat16):
    loudness = steps_of(own_key, dims, split, -0.22, 0.18) if split else 1.0
    drawn = jax.random.normal(own_key, dims, jnp.float32) * scale * loudness
    return jnp.minimum(jnp.maximum(drawn, -bound), bound).astype(held_as)


def setup_inputs(seed: int = 0) -> dict:
    keys = jax.random.split(jax.random.key(seed), 2)
    orbitals = gaussian(keys[0], (BANDS, NG, NG * NG), 0.25, 1.5, ((0, 32),))
    return dict(orbitals=orbitals)


cell_edge = 59.0
screen_rate = 0.106


def screened_kernel(grid_edge):
    points = jnp.arange(grid_edge, dtype=jnp.int32)
    signed = jnp.where(points > grid_edge // 2, points - grid_edge, points)
    half_points = jnp.arange(grid_edge // 2 + 1, dtype=jnp.int32)
    squared = signed[:, None, None] ** 2 + signed[None, :, None] ** 2 + half_points[None, None, :] ** 2
    wave_sq = squared.astype(jnp.float32) * jnp.float32((2.0 * math.pi / cell_edge) ** 2)
    safe_sq = jnp.where(squared == 0, jnp.float32(1.0), wave_sq)
    screened = 4.0 * math.pi * (-jnp.expm1(-safe_sq / (4.0 * screen_rate ** 2))) / safe_sq
    return jnp.where(squared == 0, jnp.float32(math.pi / screen_rate ** 2), screened).astype(jnp.float32)


def reference(orbitals):
    fields = orbitals.astype(jnp.float32).reshape(BANDS, NG, NG, NG)
    kernel = screened_kernel(NG)

    def one_band(single):
        density = single[None] * fields
        spectrum = jnp.fft.rfftn(density, axes=(1, 2, 3))
        potential = jnp.fft.irfftn(spectrum * kernel, s=(NG, NG, NG), axes=(1, 2, 3))
        summed = -0.25 * jnp.sum(fields * potential, axis=0)
        return summed.reshape(NG, NG * NG).astype(jnp.float32)

    return lax.map(one_band, fields)
```

```python
import math

import jax
import jax.numpy as jnp
import numpy as np
from jax import lax
from jax.experimental import pallas as pl
from jax.experimental.pallas import tpu as pltpu
from jax.sharding import PartitionSpec as P

MESH = pl.DeviceIdType.MESH
F32 = jnp.float32
BF16 = jnp.bfloat16

cell_edge = 59.0
screen_rate = 0.106

NG = 48
CELLS = NG * NG
HALF = 64
ROWS = 12
SLAB = 72


def tables():
    n = np.arange(NG)
    basis = np.zeros((NG, NG))
    basis[0] = 1.0 / math.sqrt(NG)
    for k in range(1, NG // 2):
        basis[k] = math.sqrt(2.0 / NG) * np.cos(2.0 * math.pi * ((k * n) % NG) / NG)
        basis[NG // 2 + k] = math.sqrt(2.0 / NG) * np.sin(2.0 * math.pi * ((k * n) % NG) / NG)
    basis[NG // 2] = np.cos(math.pi * n) / math.sqrt(NG)
    high = basis.astype(jnp.bfloat16).astype(np.float64)
    low = (basis - high).astype(jnp.bfloat16).astype(np.float64)

    def right(h, l):
        table = np.zeros((256, 256))
        for p in range(2):
            at = slice(p * HALF, p * HALF + NG)
            table[at, at] = h
            table[at, 128 + p * HALF : 128 + p * HALF + NG] = l
            table[128 + p * HALF : 128 + p * HALF + NG, at] = h
        return table

    def left(h, l):
        table = np.zeros((NG, 256))
        table[:, : 3 * NG] = np.concatenate([h, h, l], axis=1)
        return table

    whole = [right(high.T, low.T), right(high, low), left(high, low), left(high.T, low.T)]
    return np.concatenate(whole, axis=0).astype(jnp.bfloat16)


def halves(v):
    high = v.astype(BF16)
    low = (v - high.astype(F32)).astype(BF16)
    return high, low


def dot(a, b):
    return jnp.dot(a, b, preferred_element_type=F32)


def along_lanes(v, table):
    high, low = halves(v)
    both = dot(jnp.concatenate([high, low], axis=1), table)
    return both[:, :128] + both[:, 128:]


def along_rows(v, table):
    high, low = halves(v)
    return dot(table, jnp.concatenate([high, low, high], axis=0))


def to_lanes(v, count):
    return jnp.concatenate([v[i * NG : (i + 1) * NG] for i in range(count)], axis=1)


def to_rows(v, count):
    return jnp.concatenate([v[:, i * 128 : (i + 1) * 128] for i in range(count)], axis=0)


def spread_table(offset, depth, which):
    row = lax.broadcasted_iota(jnp.int32, (depth, 256), 0)
    lane = lax.broadcasted_iota(jnp.int32, (depth, 256), 1)
    cell = lane % HALF
    wanted = offset + NG * (lane // 128) + cell
    hit = (row == wanted) & (cell < NG)
    if which is not None:
        hit = hit & ((lane // HALF) % 2 == which)
    return jnp.where(hit, 1.0, 0.0).astype(BF16)


WINDOWS = ((0, 128, 0), (0, 256, 96), (128, 256, 64), (256, 128, 32))


def spread(parts, out_ref):
    for pair, (first, depth, offset) in enumerate(WINDOWS):
        total = None
        for ref, which in parts:
            rows = jnp.concatenate(
                [ref[:, g * 384 + first : g * 384 + first + depth] for g in range(6)], axis=0
            )
            term = dot(rows, spread_table(offset, depth, which))
            total = term if total is None else total + term
        for g in range(6):
            for side in range(2):
                y = g * 8 + pair * 2 + side
                out_ref[pl.ds(y, NG, stride=NG), :] = total[
                    g * NG : (g + 1) * NG, side * 128 : (side + 1) * 128
                ]


def signed_square(k):
    m = jnp.where(k > NG // 2, k - NG // 2, k)
    return m * m


def fill_kernel(kernel_ref):
    row = lax.broadcasted_iota(jnp.int32, (NG, 128), 0)
    lane = lax.broadcasted_iota(jnp.int32, (NG, 128), 1) % HALF
    plane = signed_square(row) + signed_square(lane)

    def one(k, carry):
        squared = plane + signed_square(k)
        wave_sq = squared.astype(F32) * F32((2.0 * math.pi / cell_edge) ** 2)
        safe_sq = jnp.where(squared == 0, F32(1.0), wave_sq)
        damped = F32(1.0) - jnp.exp(-safe_sq * F32(1.0 / (4.0 * screen_rate**2)))
        screened = F32(4.0 * math.pi) * damped / safe_sq
        value = jnp.where(squared == 0, F32(math.pi / screen_rate**2), screened)
        kernel_ref[pl.ds(pl.multiple_of(k * NG, NG), NG), :] = value
        return carry

    lax.fori_loop(0, NG, one, 0)


def exchange_kernel(
    own_ref, table_ref, out_ref,
    partner, own_wide, partner_wide, field, kernel, partial,
    from_core, chip_sum, from_x, row_sum, from_y,
    in_send, in_recv, core_send, core_recv, x_send, x_recv, y_send, y_recv,
):
    blk = lax.axis_index("blk")
    off = lax.axis_index("off")
    z, y_lo = blk // 4, blk % 4
    x, y_hi, core = off // 4, (off // 2) % 2, off % 2
    y = y_hi * 4 + y_lo

    def device(x, y, z, core):
        y = lax.rem(y + 8, 8)
        z = lax.rem(z + 8, 8)
        return (z * 4 + lax.rem(y, 4), (x * 2 + y // 4) * 2 + core)

    dy = lax.rem(x + 1, 4) - 1

    def dz_of(y_hi, k):
        even = jnp.where(core == 0, -2 * k, 2 + 2 * k)
        odd = jnp.where(core == 0, 1 - 4 * k, -1 + 4 * k)
        return jnp.where(y_hi == 0, even, odd)

    sources, targets = [], []
    for k in range(2):
        sources.append(device(x, y + dy, z + dz_of(y_hi, k), core))
        ty = lax.rem(y - dy + 8, 8)
        targets.append(device(x, ty, z - dz_of(ty // 4, k), core))
    itself = (x == 0) & (y_hi == 0) & (core == 0)

    sibling = (blk, (x * 2 + y_hi) * 2 + 1 - core)
    opposite = (blk, (x * 2 + 1 - y_hi) * 2 + core)

    def at_x(cx):
        return (blk, (cx * 2 + y_hi) * 2 + core)

    barrier = pltpu.get_barrier_semaphore()

    def greet(device_id):
        pl.semaphore_signal(barrier, inc=1, device_id=device_id, device_id_type=MESH)

    @pl.when(jnp.logical_not(itself))
    def _():
        greet(sources[0])

    greet(sources[1])
    greet(sibling)
    greet(opposite)
    for s in range(3):
        greet(at_x(lax.rem(x + 1 + s, 4)))

    @pl.when(itself)
    def _():
        pl.semaphore_wait(barrier, 6)

    @pl.when(jnp.logical_not(itself))
    def _():
        pl.semaphore_wait(barrier, 7)

    inputs = [
        pltpu.make_async_remote_copy(
            src_ref=own_ref,
            dst_ref=partner.at[k],
            send_sem=in_send.at[k],
            recv_sem=in_recv.at[k],
            device_id=targets[k],
            device_id_type=MESH,
        )
        for k in range(2)
    ]

    inputs[1].start()

    @pl.when(jnp.logical_not(itself))
    def _():
        inputs[0].start()

    spread([(own_ref, None)], own_wide)
    fill_kernel(kernel)

    @pl.when(itself)
    def _():
        partner[0] = own_ref[...]

    @pl.when(jnp.logical_not(itself))
    def _():
        inputs[0].wait()

    inputs[1].wait()

    spread([(partner.at[0], 0), (partner.at[1], 1)], partner_wide)

    right_forward = table_ref.at[pl.ds(0, 256)]
    right_backward = table_ref.at[pl.ds(256, 256)]
    left_forward = table_ref.at[pl.ds(512, NG), pl.ds(0, 3 * NG)]
    left_backward = table_ref.at[pl.ds(512 + NG, NG), pl.ds(0, 3 * NG)]

    def forward(i, carry):
        at = pl.ds(pl.multiple_of(i * (ROWS * NG), ROWS * NG), ROWS * NG)
        density = own_wide[at, :] * partner_wide[at, :]
        wide = to_lanes(along_lanes(density, right_forward[...]), ROWS)
        field[at, :] = to_rows(along_rows(wide, left_forward[...]), ROWS)
        return carry

    lax.fori_loop(0, NG // ROWS, forward, 0)

    def middle(i, carry):
        columns = [
            field[pl.ds(i * ROWS + j, NG, stride=NG), :] for j in range(ROWS)
        ]
        spectrum = along_rows(jnp.concatenate(columns, axis=1), left_forward[...])
        at = pl.ds(pl.multiple_of(i * (ROWS * NG), ROWS * NG), ROWS * NG)
        spectrum = spectrum * to_lanes(kernel[at, :], ROWS)
        back = along_rows(spectrum, left_backward[...])
        for j in range(ROWS):
            field[pl.ds(i * ROWS + j, NG, stride=NG), :] = back[:, j * 128 : (j + 1) * 128]
        return carry

    lax.fori_loop(0, NG // ROWS, middle, 0)

    low_half = lax.broadcasted_iota(jnp.int32, (NG // 2, 128), 1) < HALF

    core_copies, x_copies = [], []
    for s in range(4):
        cx = lax.rem(x + 1 + s, 4)
        core_copies.append(
            pltpu.make_async_remote_copy(
                src_ref=partial.at[cx, :, 1 - core],
                dst_ref=from_core.at[s],
                send_sem=core_send.at[s],
                recv_sem=core_recv.at[s],
                device_id=sibling,
                device_id_type=MESH,
            )
        )
        if s < 3:
            x_copies.append(
                pltpu.make_async_remote_copy(
                    src_ref=chip_sum.at[s],
                    dst_ref=from_x.at[s],
                    send_sem=x_send.at[s],
                    recv_sem=x_recv.at[s],
                    device_id=at_x(cx),
                    device_id_type=MESH,
                )
            )

    def sum_cores(s):
        cx = lax.rem(x + 1 + s, 4)
        core_copies[s].wait()
        for h in range(2):
            chip_sum[s, h] = partial[cx, h, core] + from_core[s, h]
        if s < 3:
            x_copies[s].start()

    for s in range(4):
        cx = lax.rem(x + 1 + s, 4)
        at = pl.ds(pl.multiple_of(cx * (ROWS * NG), ROWS * NG), ROWS * NG)
        wide = along_rows(to_lanes(field[at, :], ROWS), left_backward[...])
        potential = along_lanes(to_rows(wide, ROWS), right_backward[...])
        terms = potential * partner_wide[at, :]
        for i in range(ROWS):
            a = terms[i * NG : i * NG + NG // 2]
            b = terms[i * NG + NG // 2 : (i + 1) * NG]
            swapped = pltpu.roll(jnp.where(low_half, b, a), HALF, 1)
            row = jnp.where(low_half, a, b) + swapped
            partial[cx, i // 6, (i // 3) % 2, pl.ds((i % 3) * 24, 24), :] = row
        core_copies[s].start()
        if s > 0:
            sum_cores(s - 1)
    sum_cores(3)

    for c in x_copies:
        c.wait()
    for h in range(2):
        row_sum[h] = (chip_sum[3, h] + from_x[0, h]) + (from_x[1, h] + from_x[2, h])

    last = pltpu.make_async_remote_copy(
        src_ref=row_sum.at[1 - y_hi],
        dst_ref=from_y,
        send_sem=y_send,
        recv_sem=y_recv,
        device_id=opposite,
        device_id_type=MESH,
    )
    last.start()
    last.wait()
    out_ref[...] = F32(-0.25) * (row_sum[y_hi] + from_y[...])


def on_device(orbitals):
    vmem = pl.BlockSpec(memory_space=pltpu.VMEM)
    wide = pltpu.VMEM((CELLS, 128), F32)
    dma = pltpu.SemaphoreType.DMA
    found = pl.pallas_call(
        exchange_kernel,
        out_shape=jax.ShapeDtypeStruct((SLAB, 128), F32),
        in_specs=[vmem, vmem],
        out_specs=vmem,
        scratch_shapes=[
            pltpu.VMEM((2, NG, CELLS), BF16),
            wide, wide, wide, wide,
            pltpu.VMEM((4, 2, 2, SLAB, 128), F32),
            pltpu.VMEM((4, 2, SLAB, 128), F32),
            pltpu.VMEM((4, 2, SLAB, 128), F32),
            pltpu.VMEM((3, 2, SLAB, 128), F32),
            pltpu.VMEM((2, SLAB, 128), F32),
            pltpu.VMEM((SLAB, 128), F32),
            dma((2,)), dma((2,)), dma((4,)), dma((4,)),
            dma((3,)), dma((3,)), dma, dma,
        ],
        compiler_params=pltpu.CompilerParams(
            collective_id=0, has_side_effects=True, vmem_limit_bytes=48 * 2**20
        ),
    )(orbitals[0], jnp.asarray(tables()))
    cells = found.reshape(3, 24, 2, HALF).transpose(0, 2, 1, 3)[..., :NG]
    return cells.reshape(1, 3, CELLS)


def solution(mesh):
    return jax.shard_map(
        on_device,
        mesh=mesh,
        in_specs=(P("blk", None, None),),
        out_specs=P("blk", "off", None),
        check_vma=False,
    )
```

```python
import math

import jax
import jax.numpy as jnp
import numpy as np
from jax import lax
from jax.experimental import pallas as pl
from jax.experimental.pallas import tpu as pltpu
from jax.sharding import PartitionSpec as P

MESH = pl.DeviceIdType.MESH
F32 = jnp.float32
BF16 = jnp.bfloat16

cell_edge = 59.0
screen_rate = 0.106

NG = 48
CELLS = NG * NG
HALF = 64
ROWS = 12
SLAB = 72
PACKED = 56
CHUNKS = 3
CHUNK = NG // CHUNKS


def tables():
    n = np.arange(NG)
    basis = np.zeros((NG, NG))
    basis[0] = 1.0 / math.sqrt(NG)
    for k in range(1, NG // 2):
        basis[k] = math.sqrt(2.0 / NG) * np.cos(2.0 * math.pi * ((k * n) % NG) / NG)
        basis[NG // 2 + k] = math.sqrt(2.0 / NG) * np.sin(2.0 * math.pi * ((k * n) % NG) / NG)
    basis[NG // 2] = np.cos(math.pi * n) / math.sqrt(NG)
    high = basis.astype(jnp.bfloat16).astype(np.float64)
    low = (basis - high).astype(jnp.bfloat16).astype(np.float64)

    def right(h, l):
        table = np.zeros((256, 256))
        for p in range(2):
            at = slice(p * HALF, p * HALF + NG)
            table[at, at] = h
            table[at, 128 + p * HALF : 128 + p * HALF + NG] = l
            table[128 + p * HALF : 128 + p * HALF + NG, at] = h
        return table

    def left(h, l):
        table = np.zeros((NG, 256))
        table[:, : 3 * NG] = np.concatenate([h, h, l], axis=1)
        return table

    whole = [right(high.T, low.T), right(high, low), left(high, low), left(high.T, low.T)]
    return np.concatenate(whole, axis=0).astype(jnp.bfloat16)


def halves(v):
    high = v.astype(BF16)
    low = (v - high.astype(F32)).astype(BF16)
    return high, low


def dot(a, b):
    return jnp.dot(a, b, preferred_element_type=F32)


def along_lanes(v, table):
    high, low = halves(v)
    both = dot(jnp.concatenate([high, low], axis=1), table)
    return both[:, :128] + both[:, 128:]


def along_rows(v, table):
    high, low = halves(v)
    return dot(table, jnp.concatenate([high, low, high], axis=0))


def to_lanes(v, count):
    return jnp.concatenate([v[i * NG : (i + 1) * NG] for i in range(count)], axis=1)


def to_rows(v, count):
    return jnp.concatenate([v[:, i * 128 : (i + 1) * 128] for i in range(count)], axis=0)


WINDOWS = ((0, 128, 0), (0, 256, 96), (128, 256, 64), (256, 128, 32))
STARTS = (0, 128, 384, 640)
SPREAD = 768


def fill_spread(spread_ref):
    for (_, depth, offset), start in zip(WINDOWS, STARTS):
        row = lax.broadcasted_iota(jnp.int32, (depth, 256), 0)
        lane = lax.broadcasted_iota(jnp.int32, (depth, 256), 1)
        cell = lane % HALF
        hit = (row == offset + NG * (lane // 128) + cell) & (cell < NG)
        second = (lane // HALF) % 2 == 1
        for which, kept in enumerate((hit & ~second, hit & second, hit)):
            spread_ref[which, start : start + depth, :] = jnp.where(kept, 1.0, 0.0).astype(BF16)


def spread(parts, spread_ref, out_ref, start, count):
    for pair, (first, depth, _) in enumerate(WINDOWS):
        total = None
        for ref, which in parts:
            rows = jnp.concatenate(
                [
                    ref[start : start + count, g * 384 + first : g * 384 + first + depth]
                    for g in range(6)
                ],
                axis=0,
            )
            term = dot(rows, spread_ref[which, STARTS[pair] : STARTS[pair] + depth, :])
            total = term if total is None else total + term
        for g in range(6):
            for side in range(2):
                y = g * 8 + pair * 2 + side
                out_ref[pl.ds(start * NG + y, count, stride=NG), :] = total[
                    g * count : (g + 1) * count, side * 128 : (side + 1) * 128
                ]


def gap_lanes(rows):
    return lax.broadcasted_iota(jnp.int32, (rows, 128), 1) % HALF >= NG


def packed(slab):
    moved = [
        pltpu.roll(slab[56 + 8 * (q // 3) : 64 + 8 * (q // 3)], NG - 16 * (q % 3), 1)
        for q in range(6)
    ]
    filled = jnp.where(gap_lanes(48), jnp.concatenate(moved, axis=0), slab[:48])
    return jnp.concatenate([filled, slab[48:56]], axis=0)


def unpacked(slab):
    place = lax.broadcasted_iota(jnp.int32, (8, 128), 1) % HALF // 16
    tiles = [slab]
    for v in range(2):
        tile = jnp.zeros((8, 128), F32)
        for q in range(3):
            piece = slab[(v * 3 + q) * 8 : (v * 3 + q) * 8 + 8]
            tile = jnp.where(place == q, pltpu.roll(piece, 80 + 16 * q, 1), tile)
        tiles.append(tile)
    return jnp.concatenate(tiles, axis=0)


def signed_square(k):
    m = jnp.where(k > NG // 2, k - NG // 2, k)
    return m * m


def fill_kernel(kernel_ref):
    row = lax.broadcasted_iota(jnp.int32, (NG, 128), 0)
    lane = lax.broadcasted_iota(jnp.int32, (NG, 128), 1) % HALF
    plane = signed_square(row) + signed_square(lane)

    def one(k, carry):
        squared = plane + signed_square(k)
        wave_sq = squared.astype(F32) * F32((2.0 * math.pi / cell_edge) ** 2)
        safe_sq = jnp.where(squared == 0, F32(1.0), wave_sq)
        damped = F32(1.0) - jnp.exp(-safe_sq * F32(1.0 / (4.0 * screen_rate**2)))
        screened = F32(4.0 * math.pi) * damped / safe_sq
        value = jnp.where(squared == 0, F32(math.pi / screen_rate**2), screened)
        kernel_ref[pl.ds(pl.multiple_of(k * NG, NG), NG), :] = value
        return carry

    lax.fori_loop(0, NG, one, 0)


def pick(index, values):
    result = values[-1]
    for i in range(len(values) - 1):
        result = jnp.where(index == i, values[i], result)
    return result


def exchange_kernel(
    own_ref, table_ref, out_ref,
    own, table, spread_ref, partner, own_wide, partner_wide, field, kernel,
    partial, from_x, row_sum, from_y,
    copy_sem, in_send, in_recv, x_send, x_recv, y_send, y_recv,
):
    blk = lax.axis_index("blk")
    off = lax.axis_index("off")
    z, y_lo = blk // 4, blk % 4
    x, y_hi, core = off // 4, (off // 2) % 2, off % 2
    y = y_hi * 4 + y_lo

    load_own = pltpu.make_async_copy(own_ref, own, copy_sem.at[0])
    load_table = pltpu.make_async_copy(table_ref, table, copy_sem.at[1])
    load_own.start()
    load_table.start()

    def device(x, y, z, core):
        y = lax.rem(y + 8, 8)
        z = lax.rem(z + 8, 8)
        return (z * 4 + lax.rem(y, 4), (x * 2 + y // 4) * 2 + core)

    sources, targets = [], []
    for k in range(2):
        dy = pick(lax.rem(core * 2 + k + x, 4), (0, 1, 2 - 4 * lax.rem(x, 2), -1))

        def dz_of(y_hi):
            even = jnp.where(core == 0, 4 * k, 2 - 4 * k)
            odd = jnp.where(core == 0, 1 - 4 * k, 3 - 4 * k)
            return jnp.where(y_hi == 0, even, odd)

        sources.append(device(x, y + dy, z + dz_of(y_hi), core))
        ty = lax.rem(y - dy + 8, 8)
        targets.append(device(x, ty, z - dz_of(ty // 4), core))
    itself = (x == 0) & (y_hi == 0) & (core == 0)
    opposite = (blk, (x * 2 + 1 - y_hi) * 2 + core)

    def neighbour(ahead, other):
        cx = lax.rem(x + ahead, 4)
        return (blk, (cx * 2 + y_hi) * 2 + (1 - core if other else core))

    around = [(ahead, other) for ahead in (1, 2, 3, 0) for other in range(2) if ahead or other]

    barrier = pltpu.get_barrier_semaphore()

    def greet(device_id):
        pl.semaphore_signal(barrier, inc=1, device_id=device_id, device_id_type=MESH)

    greet(opposite)
    greet(sources[1])

    @pl.when(jnp.logical_not(itself))
    def _():
        greet(sources[0])

    for ahead, other in around:
        greet(neighbour(ahead, other))

    @pl.when(itself)
    def _():
        pl.semaphore_wait(barrier, 9)

    @pl.when(jnp.logical_not(itself))
    def _():
        pl.semaphore_wait(barrier, 10)

    def arrival(k, c):
        at = pl.ds(c * CHUNK, CHUNK)
        return pltpu.make_async_remote_copy(
            src_ref=own_ref.at[at],
            dst_ref=partner.at[k, at],
            send_sem=in_send.at[k, c],
            recv_sem=in_recv.at[k, c],
            device_id=targets[k],
            device_id_type=MESH,
        )

    for c in range(CHUNKS):
        arrival(1, c).start()

        @pl.when(jnp.logical_not(itself))
        def _():
            arrival(0, c).start()

    fill_spread(spread_ref)
    load_own.wait()
    spread([(own, 2)], spread_ref, own_wide, 0, NG)
    fill_kernel(kernel)
    load_table.wait()

    right_forward = table.at[pl.ds(0, 256)]
    right_backward = table.at[pl.ds(256, 256)]
    left_forward = table.at[pl.ds(512, NG), pl.ds(0, 3 * NG)]
    left_backward = table.at[pl.ds(512 + NG, NG), pl.ds(0, 3 * NG)]

    @pl.when(itself)
    def _():
        partner[0] = own[...]

    for c in range(CHUNKS):

        @pl.when(jnp.logical_not(itself))
        def _():
            arrival(0, c).wait()

        arrival(1, c).wait()
        spread([(partner.at[0], 0), (partner.at[1], 1)], spread_ref, partner_wide, c * CHUNK, CHUNK)
        at = pl.ds(c * CHUNK * NG, CHUNK * NG)
        density = own_wide[at, :] * partner_wide[at, :]
        wide = to_lanes(along_lanes(density, right_forward[...]), CHUNK)
        field[at, :] = to_rows(along_rows(wide, left_forward[...]), CHUNK)

    def middle(i, carry):
        columns = [field[pl.ds(i * ROWS + j, NG, stride=NG), :] for j in range(ROWS)]
        spectrum = along_rows(jnp.concatenate(columns, axis=1), left_forward[...])
        at = pl.ds(pl.multiple_of(i * (ROWS * NG), ROWS * NG), ROWS * NG)
        spectrum = spectrum * to_lanes(kernel[at, :], ROWS)
        back = along_rows(spectrum, left_backward[...])
        for j in range(ROWS):
            field[pl.ds(i * ROWS + j, NG, stride=NG), :] = back[:, j * 128 : (j + 1) * 128]
        return carry

    lax.fori_loop(0, NG // ROWS, middle, 0)

    def departure(h, ahead, other):
        return pltpu.make_async_remote_copy(
            src_ref=partial.at[h, ahead, other],
            dst_ref=from_x.at[h, (4 - ahead) % 4, other],
            send_sem=x_send.at[h, ahead, other],
            recv_sem=x_recv.at[h, (4 - ahead) % 4, other],
            device_id=neighbour(ahead, other),
            device_id_type=MESH,
        )

    low_half = lax.broadcasted_iota(jnp.int32, (NG // 2, 128), 1) < HALF

    for h in range(2):
        kept_hi = 1 - y_hi if h == 0 else y_hi
        for pair in ((1, 2), (3, 0)):
            starts = [
                pl.multiple_of((lax.rem(x + ahead, 4) * 2 + kept_hi) * (6 * NG), 6 * NG)
                for ahead in pair
            ]
            spectrum = jnp.concatenate([field[pl.ds(at, 6 * NG), :] for at in starts], axis=0)
            wide = along_rows(to_lanes(spectrum, 12), left_backward[...])
            potential = along_lanes(to_rows(wide, 12), right_backward[...])
            for n, (ahead, at) in enumerate(zip(pair, starts)):
                terms = potential[n * 6 * NG : (n + 1) * 6 * NG] * partner_wide[pl.ds(at, 6 * NG), :]
                for side in range(2):
                    planes = []
                    for i in range(side * 3, side * 3 + 3):
                        a = terms[i * NG : i * NG + NG // 2]
                        b = terms[i * NG + NG // 2 : (i + 1) * NG]
                        swapped = pltpu.roll(jnp.where(low_half, b, a), HALF, 1)
                        planes.append(jnp.where(low_half, a, b) + swapped)
                    other = jnp.where(core == side, 0, 1)
                    partial[h, ahead, other] = packed(jnp.concatenate(planes, axis=0))
                for other in range(2):
                    if ahead or other:
                        departure(h, ahead, other).start()

    def gathered(h):
        total = partial[h, 0, 0]
        for ahead, other in around:
            departure(h, ahead, other).wait()
        for ahead, other in around:
            total = total + from_x[h, ahead, other]
        return total

    row_sum[...] = gathered(0)
    last = pltpu.make_async_remote_copy(
        src_ref=row_sum,
        dst_ref=from_y,
        send_sem=y_send,
        recv_sem=y_recv,
        device_id=opposite,
        device_id_type=MESH,
    )
    last.start()
    kept = gathered(1)
    last.wait()
    out_ref[...] = unpacked(F32(-0.25) * (kept + from_y[...]))


def on_device(orbitals):
    anywhere = pl.BlockSpec(memory_space=pl.ANY)
    wide = pltpu.VMEM((CELLS, 128), F32)
    slab = (PACKED, 128)
    dma = pltpu.SemaphoreType.DMA
    constants = jnp.asarray(tables())
    found = pl.pallas_call(
        exchange_kernel,
        out_shape=jax.ShapeDtypeStruct((SLAB, 128), F32),
        in_specs=[anywhere, anywhere],
        out_specs=pl.BlockSpec(memory_space=pltpu.VMEM),
        scratch_shapes=[
            pltpu.VMEM((NG, CELLS), BF16),
            pltpu.VMEM(constants.shape, BF16),
            pltpu.VMEM((3, SPREAD, 256), BF16),
            pltpu.VMEM((2, NG, CELLS), BF16),
            wide, wide, wide, wide,
            pltpu.VMEM((2, 4, 2, *slab), F32),
            pltpu.VMEM((2, 4, 2, *slab), F32),
            pltpu.VMEM(slab, F32),
            pltpu.VMEM(slab, F32),
            dma((2,)),
            dma((2, CHUNKS)), dma((2, CHUNKS)),
            dma((2, 4, 2)), dma((2, 4, 2)),
            dma, dma,
        ],
        compiler_params=pltpu.CompilerParams(
            collective_id=0, has_side_effects=True, vmem_limit_bytes=60 * 2**20
        ),
    )(orbitals[0], constants)
    cells = found.reshape(3, 24, 2, HALF).transpose(0, 2, 1, 3)[..., :NG]
    return cells.reshape(1, 3, CELLS)


def solution(mesh):
    return jax.shard_map(
        on_device,
        mesh=mesh,
        in_specs=(P("blk", None, None),),
        out_specs=P("blk", "off", None),
        check_vma=False,
    )
```

```python
import math

import jax
import jax.numpy as jnp
import numpy as np
from jax import lax
from jax.experimental import pallas as pl
from jax.experimental.pallas import tpu as pltpu
from jax.sharding import PartitionSpec as P

MESH = pl.DeviceIdType.MESH
F32 = jnp.float32
BF16 = jnp.bfloat16

cell_edge = 59.0
screen_rate = 0.106

NG = 48
CELLS = NG * NG
HALF = 64
ROWS = 12
SLAB = 72
PACKED = 56
EARLY = 3
CHUNKS = 3
CHUNK = NG // CHUNKS


def tables():
    n = np.arange(NG)
    basis = np.zeros((NG, NG))
    basis[0] = 1.0 / math.sqrt(NG)
    for k in range(1, NG // 2):
        basis[k] = math.sqrt(2.0 / NG) * np.cos(2.0 * math.pi * ((k * n) % NG) / NG)
        basis[NG // 2 + k] = math.sqrt(2.0 / NG) * np.sin(2.0 * math.pi * ((k * n) % NG) / NG)
    basis[NG // 2] = np.cos(math.pi * n) / math.sqrt(NG)
    high = basis.astype(jnp.bfloat16).astype(np.float64)
    low = (basis - high).astype(jnp.bfloat16).astype(np.float64)

    def right(h, l):
        table = np.zeros((256, 256))
        for p in range(2):
            at = slice(p * HALF, p * HALF + NG)
            table[at, at] = h
            table[at, 128 + p * HALF : 128 + p * HALF + NG] = l
            table[128 + p * HALF : 128 + p * HALF + NG, at] = h
        return table

    def left(h, l):
        table = np.zeros((NG, 256))
        table[:, : 3 * NG] = np.concatenate([h, h, l], axis=1)
        return table

    whole = [right(high.T, low.T), right(high, low), left(high, low), left(high.T, low.T)]
    return np.concatenate(whole, axis=0).astype(jnp.bfloat16)


def halves(v):
    high = v.astype(BF16)
    low = (v - high.astype(F32)).astype(BF16)
    return high, low


def dot(a, b):
    return jnp.dot(a, b, preferred_element_type=F32)


def along_lanes(v, table):
    high, low = halves(v)
    both = dot(jnp.concatenate([high, low], axis=1), table)
    return both[:, :128] + both[:, 128:]


def along_rows(v, table):
    high, low = halves(v)
    return dot(table, jnp.concatenate([high, low, high], axis=0))


def to_lanes(v, count):
    return jnp.concatenate([v[i * NG : (i + 1) * NG] for i in range(count)], axis=1)


def to_rows(v, count):
    return jnp.concatenate([v[:, i * 128 : (i + 1) * 128] for i in range(count)], axis=0)


WINDOWS = ((0, 128, 0), (0, 256, 96), (128, 256, 64), (256, 128, 32))
STARTS = (0, 128, 384, 640)
SPREAD = 768


def fill_spread(spread_ref):
    for (_, depth, offset), start in zip(WINDOWS, STARTS):
        row = lax.broadcasted_iota(jnp.int32, (depth, 256), 0)
        lane = lax.broadcasted_iota(jnp.int32, (depth, 256), 1)
        cell = lane % HALF
        hit = (row == offset + NG * (lane // 128) + cell) & (cell < NG)
        second = (lane // HALF) % 2 == 1
        for which, kept in enumerate((hit & ~second, hit & second, hit)):
            spread_ref[which, start : start + depth, :] = jnp.where(kept, 1.0, 0.0).astype(BF16)


def spread(parts, spread_ref, out_ref, start, count):
    for pair, (first, depth, _) in enumerate(WINDOWS):
        total = None
        for ref, which in parts:
            rows = jnp.concatenate(
                [
                    ref[start : start + count, g * 384 + first : g * 384 + first + depth]
                    for g in range(6)
                ],
                axis=0,
            )
            term = dot(rows, spread_ref[which, STARTS[pair] : STARTS[pair] + depth, :])
            total = term if total is None else total + term
        for g in range(6):
            for side in range(2):
                y = g * 8 + pair * 2 + side
                out_ref[pl.ds(start * NG + y, count, stride=NG), :] = total[
                    g * count : (g + 1) * count, side * 128 : (side + 1) * 128
                ]


def gap_lanes(rows):
    return lax.broadcasted_iota(jnp.int32, (rows, 128), 1) % HALF >= NG


def packed(slab):
    moved = [
        pltpu.roll(slab[56 + 8 * (q // 3) : 64 + 8 * (q // 3)], NG - 16 * (q % 3), 1)
        for q in range(6)
    ]
    filled = jnp.where(gap_lanes(48), jnp.concatenate(moved, axis=0), slab[:48])
    return jnp.concatenate([filled, slab[48:56]], axis=0)


def unpacked(slab):
    place = lax.broadcasted_iota(jnp.int32, (8, 128), 1) % HALF // 16
    tiles = [slab]
    for v in range(2):
        tile = jnp.zeros((8, 128), F32)
        for q in range(3):
            piece = slab[(v * 3 + q) * 8 : (v * 3 + q) * 8 + 8]
            tile = jnp.where(place == q, pltpu.roll(piece, 80 + 16 * q, 1), tile)
        tiles.append(tile)
    return jnp.concatenate(tiles, axis=0)


def signed_square(k):
    m = jnp.where(k > NG // 2, k - NG // 2, k)
    return m * m


def fill_kernel(kernel_ref):
    row = lax.broadcasted_iota(jnp.int32, (NG, 128), 0)
    lane = lax.broadcasted_iota(jnp.int32, (NG, 128), 1) % HALF
    plane = signed_square(row) + signed_square(lane)

    def one(k, carry):
        squared = plane + signed_square(k)
        wave_sq = squared.astype(F32) * F32((2.0 * math.pi / cell_edge) ** 2)
        safe_sq = jnp.where(squared == 0, F32(1.0), wave_sq)
        damped = F32(1.0) - jnp.exp(-safe_sq * F32(1.0 / (4.0 * screen_rate**2)))
        screened = F32(4.0 * math.pi) * damped / safe_sq
        value = jnp.where(squared == 0, F32(math.pi / screen_rate**2), screened)
        kernel_ref[pl.ds(pl.multiple_of(k * NG, NG), NG), :] = value
        return carry

    lax.fori_loop(0, NG, one, 0)


def join_rows(planes_ref, out_ref):
    lane = lax.broadcasted_iota(jnp.int32, (3, 128), 1)
    full = [None] * (CELLS // 128)
    for y in range(NG):
        row = planes_ref[pl.ds(y % 24, 3, stride=24), :]
        tile, at = divmod(y * NG, 128)
        row = pltpu.roll(row, (at - HALF * (y // 24)) % 128, 1)
        full[tile] = row if at == 0 else jnp.where(lane < at, full[tile], row)
        if at + NG > 128:
            full[tile + 1] = row
    for tile, row in enumerate(full):
        for plane in range(3):
            out_ref[plane, :, tile * 128 : (tile + 1) * 128] = row[plane : plane + 1]


def pick(index, values):
    result = values[-1]
    for i in range(len(values) - 1):
        result = jnp.where(index == i, values[i], result)
    return result


def exchange_kernel(
    own_ref, table_ref, out_ref,
    own, table, spread_ref, partner, own_wide, partner_wide, field, kernel,
    partial, from_x, row_sum, from_y,
    planes_ref, copy_sem, in_send, in_recv, x_send, x_recv, y_send, y_recv, opposite_sem, go_sem,
):
    blk = lax.axis_index("blk")
    off = lax.axis_index("off")
    z, y_lo = blk // 4, blk % 4
    x, y_hi, core = off // 4, (off // 2) % 2, off % 2
    y = y_hi * 4 + y_lo

    load_own = pltpu.make_async_copy(own_ref, own, copy_sem.at[0])
    load_table = pltpu.make_async_copy(table_ref, table, copy_sem.at[1])
    load_own.start()
    load_table.start()

    def device(x, y, z, core):
        y = lax.rem(y + 8, 8)
        z = lax.rem(z + 8, 8)
        return (z * 4 + lax.rem(y, 4), (x * 2 + y // 4) * 2 + core)

    sources, targets = [], []
    for k in range(2):
        dy = pick(lax.rem(core * 2 + k + x, 4), (0, 1, 2 - 4 * lax.rem(x, 2), -1))

        def dz_of(y_hi):
            even = jnp.where(core == 0, 4 * k, 2 - 4 * k)
            odd = jnp.where(core == 0, 1 - 4 * k, 3 - 4 * k)
            return jnp.where(y_hi == 0, even, odd)

        sources.append(device(x, y + dy, z + dz_of(y_hi), core))
        ty = lax.rem(y - dy + 8, 8)
        targets.append(device(x, ty, z - dz_of(ty // 4), core))
    itself = (x == 0) & (y_hi == 0) & (core == 0)
    opposite = (blk, (x * 2 + 1 - y_hi) * 2 + core)

    def neighbour(ahead, other):
        cx = lax.rem(x + ahead, 4)
        return (blk, (cx * 2 + y_hi) * 2 + (1 - core if other else core))

    around = [(ahead, other) for ahead in (1, 2, 3, 0) for other in range(2) if ahead or other]

    barrier = pltpu.get_barrier_semaphore()

    def greet(device_id):
        pl.semaphore_signal(barrier, inc=1, device_id=device_id, device_id_type=MESH)

    below, above = device(x, y - 2, z, core), device(x, y + 2, z, core)
    greet(below)
    greet(above)
    for ahead, other in around:
        greet(neighbour(ahead, other))

    mine_early = z < EARLY
    moves = (jnp.logical_not(itself), itself | True)
    to_early = [target[0] // 4 < EARLY for target in targets]
    from_early = [source[0] // 4 < EARLY for source in sources]
    defer_to = [moves[k] & mine_early & jnp.logical_not(to_early[k]) for k in range(2)]
    defer_from = [moves[k] & jnp.logical_not(mine_early) & from_early[k] for k in range(2)]
    greetings = 9
    for k in range(2):

        @pl.when(moves[k] & jnp.logical_not(defer_from[k]))
        def _():
            greet(sources[k])

        @pl.when(defer_to[k])
        def _():
            greet(targets[k])

        greetings = greetings + jnp.where(moves[k] & jnp.logical_not(defer_to[k]), 1, 0)
        greetings = greetings + jnp.where(defer_from[k], 1, 0)

    pl.semaphore_wait(barrier, greetings)

    for k in range(2):

        @pl.when(defer_from[k])
        def _():
            pl.semaphore_signal(
                go_sem.at[k], inc=1, device_id=sources[k], device_id_type=MESH
            )

    def arrival(k, c):
        at = pl.ds(c * CHUNK, CHUNK)
        return pltpu.make_async_remote_copy(
            src_ref=own_ref.at[at],
            dst_ref=partner.at[k, at],
            send_sem=in_send.at[k, c],
            recv_sem=in_recv.at[k, c],
            device_id=targets[k],
            device_id_type=MESH,
        )

    later = [
        moves[k] & jnp.logical_not(mine_early | to_early[k]) & to_early[1 - k]
        for k in range(2)
    ]
    for c in range(CHUNKS):
        for k in range(2):

            @pl.when(moves[k] & jnp.logical_not(defer_to[k] | later[k]))
            def _():
                arrival(k, c).start()

    pl.semaphore_signal(opposite_sem, inc=1, device_id=below, device_id_type=MESH)
    fill_spread(spread_ref)
    load_own.wait()
    spread([(own, 2)], spread_ref, own_wide, 0, NG)
    fill_kernel(kernel)
    load_table.wait()

    for k in range(2):

        @pl.when(defer_to[k])
        def _():
            pl.semaphore_wait(go_sem.at[k], 1)
            for c in range(CHUNKS):
                arrival(k, c).start()

        @pl.when(later[k])
        def _():
            for c in range(CHUNKS):
                arrival(1 - k, c).wait_send()
            for c in range(CHUNKS):
                arrival(k, c).start()

    right_forward = table.at[pl.ds(0, 256)]
    right_backward = table.at[pl.ds(256, 256)]
    left_forward = table.at[pl.ds(512, NG), pl.ds(0, 3 * NG)]
    left_backward = table.at[pl.ds(512 + NG, NG), pl.ds(0, 3 * NG)]

    @pl.when(itself)
    def _():
        partner[0] = own[...]

    for c in range(CHUNKS):

        @pl.when(moves[0])
        def _():
            arrival(0, c).wait_recv()

        arrival(1, c).wait_recv()
        spread([(partner.at[0], 0), (partner.at[1], 1)], spread_ref, partner_wide, c * CHUNK, CHUNK)
        at = pl.ds(c * CHUNK * NG, CHUNK * NG)
        density = own_wide[at, :] * partner_wide[at, :]
        wide = to_lanes(along_lanes(density, right_forward[...]), CHUNK)
        field[at, :] = to_rows(along_rows(wide, left_forward[...]), CHUNK)

    def middle(i, carry):
        columns = [field[pl.ds(i * ROWS + j, NG, stride=NG), :] for j in range(ROWS)]
        spectrum = along_rows(jnp.concatenate(columns, axis=1), left_forward[...])
        at = pl.ds(pl.multiple_of(i * (ROWS * NG), ROWS * NG), ROWS * NG)
        spectrum = spectrum * to_lanes(kernel[at, :], ROWS)
        back = along_rows(spectrum, left_backward[...])
        for j in range(ROWS):
            field[pl.ds(i * ROWS + j, NG, stride=NG), :] = back[:, j * 128 : (j + 1) * 128]
        return carry

    lax.fori_loop(0, NG // ROWS, middle, 0)

    def departure(h, ahead, other):
        return pltpu.make_async_remote_copy(
            src_ref=partial.at[h, ahead, other],
            dst_ref=from_x.at[h, (4 - ahead) % 4, other],
            send_sem=x_send.at[h, ahead, other],
            recv_sem=x_recv.at[h, (4 - ahead) % 4, other],
            device_id=neighbour(ahead, other),
            device_id_type=MESH,
        )

    low_half = lax.broadcasted_iota(jnp.int32, (NG // 2, 128), 1) < HALF

    for h in range(2):
        kept_hi = 1 - y_hi if h == 0 else y_hi
        for pair in ((1, 2), (3, 0)):
            starts = [
                pl.multiple_of((lax.rem(x + ahead, 4) * 2 + kept_hi) * (6 * NG), 6 * NG)
                for ahead in pair
            ]
            spectrum = jnp.concatenate([field[pl.ds(at, 6 * NG), :] for at in starts], axis=0)
            wide = along_rows(to_lanes(spectrum, 12), left_backward[...])
            potential = along_lanes(to_rows(wide, 12), right_backward[...])
            for n, (ahead, at) in enumerate(zip(pair, starts)):
                terms = potential[n * 6 * NG : (n + 1) * 6 * NG] * partner_wide[pl.ds(at, 6 * NG), :]
                for side in range(2):
                    planes = []
                    for i in range(side * 3, side * 3 + 3):
                        a = terms[i * NG : i * NG + NG // 2]
                        b = terms[i * NG + NG // 2 : (i + 1) * NG]
                        swapped = pltpu.roll(jnp.where(low_half, b, a), HALF, 1)
                        planes.append(jnp.where(low_half, a, b) + swapped)
                    other = jnp.where(core == side, 0, 1)
                    partial[h, ahead, other] = packed(jnp.concatenate(planes, axis=0))
                for other in range(2):
                    if ahead or other:
                        departure(h, ahead, other).start()

    def gathered(h):
        total = partial[h, 0, 0]
        for ahead, other in around:
            departure(h, ahead, other).wait()
        for ahead, other in around:
            total = total + from_x[h, ahead, other]
        return total

    row_sum[...] = gathered(0)
    pl.semaphore_wait(opposite_sem, 1)
    last = pltpu.make_async_remote_copy(
        src_ref=row_sum,
        dst_ref=from_y,
        send_sem=y_send,
        recv_sem=y_recv,
        device_id=opposite,
        device_id_type=MESH,
    )
    last.start()
    kept = gathered(1)

    for k in range(2):

        @pl.when(moves[k] & jnp.logical_not(later[1 - k]))
        def _():
            for c in range(CHUNKS):
                arrival(k, c).wait_send()

    last.wait()
    planes_ref[...] = unpacked(F32(-0.25) * (kept + from_y[...]))
    join_rows(planes_ref, out_ref)


def on_device(orbitals):
    anywhere = pl.BlockSpec(memory_space=pl.ANY)
    wide = pltpu.VMEM((CELLS, 128), F32)
    slab = (PACKED, 128)
    dma = pltpu.SemaphoreType.DMA
    constants = jnp.asarray(tables())
    found = pl.pallas_call(
        exchange_kernel,
        out_shape=jax.ShapeDtypeStruct((3, 1, CELLS), F32),
        in_specs=[anywhere, anywhere],
        out_specs=pl.BlockSpec(memory_space=pltpu.VMEM),
        scratch_shapes=[
            pltpu.VMEM((NG, CELLS), BF16),
            pltpu.VMEM(constants.shape, BF16),
            pltpu.VMEM((3, SPREAD, 256), BF16),
            pltpu.VMEM((2, NG, CELLS), BF16),
            wide, wide, wide, wide,
            pltpu.VMEM((2, 4, 2, *slab), F32),
            pltpu.VMEM((2, 4, 2, *slab), F32),
            pltpu.VMEM(slab, F32),
            pltpu.VMEM(slab, F32),
            pltpu.VMEM((SLAB, 128), F32),
            dma((2,)),
            dma((2, CHUNKS)), dma((2, CHUNKS)),
            dma((2, 4, 2)), dma((2, 4, 2)),
            dma, dma,
            pltpu.SemaphoreType.REGULAR,
            pltpu.SemaphoreType.REGULAR((2,)),
        ],
        compiler_params=pltpu.CompilerParams(
            collective_id=0, has_side_effects=True, vmem_limit_bytes=54 * 2**20 - 2**17
        ),
    )(orbitals[0], constants)
    return found.transpose(1, 0, 2)


def solution(mesh):
    return jax.shard_map(
        on_device,
        mesh=mesh,
        in_specs=(P("blk", None, None),),
        out_specs=P("blk", "off", None),
        check_vma=False,
    )
```

```python
import math

import jax
import jax.numpy as jnp
import numpy as np
from jax import lax
from jax.experimental import pallas as pl
from jax.experimental.pallas import tpu as pltpu
from jax.sharding import PartitionSpec as P

MESH = pl.DeviceIdType.MESH
F32 = jnp.float32
BF16 = jnp.bfloat16

cell_edge = 59.0
screen_rate = 0.106

NG = 48
CELLS = NG * NG
HALF = 64
SLAB = 72
PACKED = 56
EARLY = 4
CHUNKS = 3
CHUNK = NG // CHUNKS


def tables():
    n = np.arange(NG)
    basis = np.zeros((NG, NG))
    basis[0] = 1.0 / math.sqrt(NG)
    for k in range(1, NG // 2):
        basis[k] = math.sqrt(2.0 / NG) * np.cos(2.0 * math.pi * ((k * n) % NG) / NG)
        basis[NG // 2 + k] = math.sqrt(2.0 / NG) * np.sin(2.0 * math.pi * ((k * n) % NG) / NG)
    basis[NG // 2] = np.cos(math.pi * n) / math.sqrt(NG)
    high = basis.astype(jnp.bfloat16).astype(np.float64)
    low = (basis - high).astype(jnp.bfloat16).astype(np.float64)

    def right(h, l):
        table = np.zeros((256, 256))
        for p in range(2):
            at = slice(p * HALF, p * HALF + NG)
            table[at, at] = h
            table[at, 128 + p * HALF : 128 + p * HALF + NG] = l
            table[128 + p * HALF : 128 + p * HALF + NG, at] = h
        return table

    def left(h, l):
        table = np.zeros((NG, 256))
        table[:, : 3 * NG] = np.concatenate([h, h, l], axis=1)
        return table

    whole = [right(high.T, low.T), right(high, low), left(high, low), left(high.T, low.T)]
    return np.concatenate(whole, axis=0).astype(jnp.bfloat16)


def halves(v):
    high = v.astype(BF16)
    low = (v - high.astype(F32)).astype(BF16)
    return high, low


def dot(a, b):
    return jnp.dot(a, b, preferred_element_type=F32)


def along_lanes(v, table):
    high, low = halves(v)
    both = dot(jnp.concatenate([high, low], axis=1), table)
    return both[:, :128] + both[:, 128:]


def along_rows(v, table):
    high, low = halves(v)
    return dot(table, jnp.concatenate([high, low, high], axis=0))


def to_lanes(v, count):
    return jnp.concatenate([v[i * NG : (i + 1) * NG] for i in range(count)], axis=1)


def to_rows(v, count):
    return jnp.concatenate([v[:, i * 128 : (i + 1) * 128] for i in range(count)], axis=0)


WINDOWS = ((0, 128, 0), (0, 256, 96), (128, 256, 64), (256, 128, 32))
STARTS = (0, 128, 384, 640)
SPREAD = 768


def fill_spread(spread_ref):
    for (_, depth, offset), start in zip(WINDOWS, STARTS):
        row = lax.broadcasted_iota(jnp.int32, (depth, 256), 0)
        lane = lax.broadcasted_iota(jnp.int32, (depth, 256), 1)
        cell = lane % HALF
        hit = (row == offset + NG * (lane // 128) + cell) & (cell < NG)
        second = (lane // HALF) % 2 == 1
        for which, kept in enumerate((hit & ~second, hit & second, hit)):
            spread_ref[which, start : start + depth, :] = jnp.where(kept, 1.0, 0.0).astype(BF16)


def spread(parts, spread_ref, out_ref, start, count):
    for pair, (first, depth, _) in enumerate(WINDOWS):
        total = None
        for ref, which in parts:
            rows = jnp.concatenate(
                [
                    ref[start : start + count, g * 384 + first : g * 384 + first + depth]
                    for g in range(6)
                ],
                axis=0,
            )
            term = dot(rows, spread_ref[which, STARTS[pair] : STARTS[pair] + depth, :])
            total = term if total is None else total + term
        for g in range(6):
            for side in range(2):
                y = g * 8 + pair * 2 + side
                out_ref[pl.ds(start * NG + y, count, stride=NG), :] = total[
                    g * count : (g + 1) * count, side * 128 : (side + 1) * 128
                ]


def gap_lanes(rows):
    return lax.broadcasted_iota(jnp.int32, (rows, 128), 1) % HALF >= NG


def packed(slab):
    moved = [
        pltpu.roll(slab[56 + 8 * (q // 3) : 64 + 8 * (q // 3)], NG - 16 * (q % 3), 1)
        for q in range(6)
    ]
    filled = jnp.where(gap_lanes(48), jnp.concatenate(moved, axis=0), slab[:48])
    return jnp.concatenate([filled, slab[48:56]], axis=0)


def unpacked(slab):
    place = lax.broadcasted_iota(jnp.int32, (8, 128), 1) % HALF // 16
    tiles = [slab]
    for v in range(2):
        tile = jnp.zeros((8, 128), F32)
        for q in range(3):
            piece = slab[(v * 3 + q) * 8 : (v * 3 + q) * 8 + 8]
            tile = jnp.where(place == q, pltpu.roll(piece, 80 + 16 * q, 1), tile)
        tiles.append(tile)
    return jnp.concatenate(tiles, axis=0)


def signed_square(k):
    m = jnp.where(k > NG // 2, k - NG // 2, k)
    return m * m


def fill_kernel(kernel_ref):
    row = lax.broadcasted_iota(jnp.int32, (NG, 128), 0)
    lane = lax.broadcasted_iota(jnp.int32, (NG, 128), 1) % HALF
    plane = signed_square(row) + signed_square(lane)

    def one(k, carry):
        squared = plane + signed_square(k)
        wave_sq = squared.astype(F32) * F32((2.0 * math.pi / cell_edge) ** 2)
        safe_sq = jnp.where(squared == 0, F32(1.0), wave_sq)
        damped = F32(1.0) - jnp.exp(-safe_sq * F32(1.0 / (4.0 * screen_rate**2)))
        screened = F32(4.0 * math.pi) * damped / safe_sq
        value = jnp.where(squared == 0, F32(math.pi / screen_rate**2), screened)
        kernel_ref[pl.ds(pl.multiple_of(k * NG, NG), NG), :] = value
        return carry

    lax.fori_loop(0, NG, one, 0)


def join_rows(planes_ref, out_ref):
    lane = lax.broadcasted_iota(jnp.int32, (3, 128), 1)
    full = [None] * (CELLS // 128)
    for y in range(NG):
        row = planes_ref[pl.ds(y % 24, 3, stride=24), :]
        tile, at = divmod(y * NG, 128)
        row = pltpu.roll(row, (at - HALF * (y // 24)) % 128, 1)
        full[tile] = row if at == 0 else jnp.where(lane < at, full[tile], row)
        if at + NG > 128:
            full[tile + 1] = row
    for tile, row in enumerate(full):
        for plane in range(3):
            out_ref[plane, :, tile * 128 : (tile + 1) * 128] = row[plane : plane + 1]


def pick(index, values):
    result = values[-1]
    for i in range(len(values) - 1):
        result = jnp.where(index == i, values[i], result)
    return result


def exchange_kernel(
    own_ref, table_ref, out_ref,
    own, table, spread_ref, partner, own_wide, partner_wide, field, kernel,
    partial, from_x, row_sum, from_y,
    planes_ref, copy_sem, in_send, in_recv, x_send, x_recv, y_send, y_recv, opposite_sem, go_sem,
):
    blk = lax.axis_index("blk")
    off = lax.axis_index("off")
    z, y_lo = blk // 4, blk % 4
    x, y_hi, core = off // 4, (off // 2) % 2, off % 2
    y = y_hi * 4 + y_lo

    load_own = pltpu.make_async_copy(own_ref, own, copy_sem.at[0])
    load_table = pltpu.make_async_copy(table_ref, table, copy_sem.at[1])
    load_own.start()
    load_table.start()

    def device(x, y, z, core):
        y = lax.rem(y + 8, 8)
        z = lax.rem(z + 8, 8)
        return (z * 4 + lax.rem(y, 4), (x * 2 + y // 4) * 2 + core)

    sources, targets = [], []
    for k in range(2):
        dy = pick(lax.rem(core * 2 + k + x, 4), (0, 1, 2 - 4 * lax.rem(y, 2), -1))

        def dz_of(y_hi):
            even = jnp.where(core == 0, 4 * k, 2 - 4 * k)
            odd = jnp.where(core == 0, 1 - 4 * k, 3 - 4 * k)
            return jnp.where(y_hi == 0, even, odd)

        sources.append(device(x, y + dy, z + dz_of(y_hi), core))
        ty = lax.rem(y - dy + 8, 8)
        targets.append(device(x, ty, z - dz_of(ty // 4), core))
    itself = (x == 0) & (y_hi == 0) & (core == 0)
    opposite = (blk, (x * 2 + 1 - y_hi) * 2 + core)

    def neighbour(ahead, other):
        cx = lax.rem(x + ahead, 4)
        return (blk, (cx * 2 + y_hi) * 2 + (1 - core if other else core))

    around = [(ahead, other) for ahead in (1, 2, 3, 0) for other in range(2) if ahead or other]

    barrier = pltpu.get_barrier_semaphore()

    def greet(device_id):
        pl.semaphore_signal(barrier, inc=1, device_id=device_id, device_id_type=MESH)

    below, above = device(x, y - 2, z, core), device(x, y + 2, z, core)
    greet(below)
    greet(above)
    for ahead, other in around:
        greet(neighbour(ahead, other))

    mine_early = z < EARLY
    moves = (jnp.logical_not(itself), itself | True)
    to_early = [target[0] // 4 < EARLY for target in targets]
    from_early = [source[0] // 4 < EARLY for source in sources]
    defer_to = [moves[k] & mine_early & jnp.logical_not(to_early[k]) for k in range(2)]
    defer_from = [moves[k] & jnp.logical_not(mine_early) & from_early[k] for k in range(2)]
    greetings = 9
    for k in range(2):

        @pl.when(moves[k] & jnp.logical_not(defer_from[k]))
        def _():
            greet(sources[k])

        @pl.when(defer_to[k])
        def _():
            greet(targets[k])

        greetings = greetings + jnp.where(moves[k] & jnp.logical_not(defer_to[k]), 1, 0)
        greetings = greetings + jnp.where(defer_from[k], 1, 0)

    pl.semaphore_wait(barrier, greetings)

    for k in range(2):

        @pl.when(defer_from[k])
        def _():
            pl.semaphore_signal(
                go_sem.at[k], inc=1, device_id=sources[k], device_id_type=MESH
            )

    def arrival(k, c):
        at = pl.ds(c * CHUNK, CHUNK)
        return pltpu.make_async_remote_copy(
            src_ref=own_ref.at[at],
            dst_ref=partner.at[k, at],
            send_sem=in_send.at[k, c],
            recv_sem=in_recv.at[k, c],
            device_id=targets[k],
            device_id_type=MESH,
        )

    later = [
        moves[k] & jnp.logical_not(mine_early | to_early[k]) & to_early[1 - k]
        for k in range(2)
    ]
    for c in range(CHUNKS):
        for k in range(2):

            @pl.when(moves[k] & jnp.logical_not(defer_to[k] | later[k]))
            def _():
                arrival(k, c).start()

    pl.semaphore_signal(opposite_sem, inc=1, device_id=below, device_id_type=MESH)
    fill_spread(spread_ref)
    load_own.wait()
    spread([(own, 2)], spread_ref, own_wide, 0, NG)
    fill_kernel(kernel)
    load_table.wait()

    for k in range(2):

        @pl.when(defer_to[k])
        def _():
            pl.semaphore_wait(go_sem.at[k], 1)
            for c in range(CHUNKS):
                arrival(k, c).start()

        @pl.when(later[k])
        def _():
            for c in range(CHUNKS):
                arrival(1 - k, c).wait_send()
            for c in range(CHUNKS):
                arrival(k, c).start()

    right_forward = table.at[pl.ds(0, 256)]
    right_backward = table.at[pl.ds(256, 256)]
    left_forward = table.at[pl.ds(512, NG), pl.ds(0, 3 * NG)]
    left_backward = table.at[pl.ds(512 + NG, NG), pl.ds(0, 3 * NG)]

    @pl.when(itself)
    def _():
        partner[0] = own[...]

    for c in range(CHUNKS):

        @pl.when(moves[0])
        def _():
            arrival(0, c).wait_recv()

        arrival(1, c).wait_recv()
        spread([(partner.at[0], 0), (partner.at[1], 1)], spread_ref, partner_wide, c * CHUNK, CHUNK)
        at = pl.ds(c * CHUNK * NG, CHUNK * NG)
        density = own_wide[at, :] * partner_wide[at, :]
        wide = to_lanes(along_lanes(density, right_forward[...]), CHUNK)
        field[at, :] = to_rows(along_rows(wide, left_forward[...]), CHUNK)

    columns = [field[pl.ds(j, NG, stride=NG), :] for j in range(NG)]
    spectrum = along_rows(jnp.concatenate(columns, axis=1), left_forward[...])
    back = along_rows(spectrum * to_lanes(kernel[...], NG), left_backward[...])
    for j in range(NG):
        field[pl.ds(j, NG, stride=NG), :] = back[:, j * 128 : (j + 1) * 128]

    def departure(h, ahead, other):
        return pltpu.make_async_remote_copy(
            src_ref=partial.at[h, ahead, other],
            dst_ref=from_x.at[h, (4 - ahead) % 4, other],
            send_sem=x_send.at[h, ahead, other],
            recv_sem=x_recv.at[h, (4 - ahead) % 4, other],
            device_id=neighbour(ahead, other),
            device_id_type=MESH,
        )

    low_half = lax.broadcasted_iota(jnp.int32, (NG // 2, 128), 1) < HALF

    def slabs(h):
        kept_hi = 1 - y_hi if h == 0 else y_hi
        starts = [
            pl.multiple_of((lax.rem(x + ahead, 4) * 2 + kept_hi) * (6 * NG), 6 * NG)
            for ahead in range(4)
        ]
        spectrum = jnp.concatenate([field[pl.ds(at, 6 * NG), :] for at in starts], axis=0)
        wide = along_rows(to_lanes(spectrum, 24), left_backward[...])
        potential = along_lanes(to_rows(wide, 24), right_backward[...])
        for ahead in (2, 1, 3, 0):
            terms = (
                potential[ahead * 6 * NG : (ahead + 1) * 6 * NG]
                * partner_wide[pl.ds(starts[ahead], 6 * NG), :]
            )
            for side in range(2):
                planes = []
                for i in range(side * 3, side * 3 + 3):
                    a = terms[i * NG : i * NG + NG // 2]
                    b = terms[i * NG + NG // 2 : (i + 1) * NG]
                    swapped = pltpu.roll(jnp.where(low_half, b, a), HALF, 1)
                    planes.append(jnp.where(low_half, a, b) + swapped)
                other = jnp.where(core == side, 0, 1)
                partial[h, ahead, other] = packed(jnp.concatenate(planes, axis=0))
            for other in range(2):
                if ahead or other:
                    departure(h, ahead, other).start()

    slabs(0)
    slabs(1)

    def gathered(h):
        total = partial[h, 0, 0]
        for ahead, other in around:
            departure(h, ahead, other).wait()
        for ahead, other in around:
            total = total + from_x[h, ahead, other]
        return total

    row_sum[...] = gathered(0)
    pl.semaphore_wait(opposite_sem, 1)
    last = pltpu.make_async_remote_copy(
        src_ref=row_sum,
        dst_ref=from_y,
        send_sem=y_send,
        recv_sem=y_recv,
        device_id=opposite,
        device_id_type=MESH,
    )
    last.start()
    kept = gathered(1)

    for k in range(2):

        @pl.when(moves[k] & jnp.logical_not(later[1 - k]))
        def _():
            for c in range(CHUNKS):
                arrival(k, c).wait_send()

    last.wait()
    planes_ref[...] = unpacked(F32(-0.25) * (kept + from_y[...]))
    join_rows(planes_ref, out_ref)


def on_device(orbitals):
    anywhere = pl.BlockSpec(memory_space=pl.ANY)
    wide = pltpu.VMEM((CELLS, 128), F32)
    slab = (PACKED, 128)
    dma = pltpu.SemaphoreType.DMA
    constants = jnp.asarray(tables())
    found = pl.pallas_call(
        exchange_kernel,
        out_shape=jax.ShapeDtypeStruct((3, 1, CELLS), F32),
        in_specs=[anywhere, anywhere],
        out_specs=pl.BlockSpec(memory_space=pltpu.VMEM),
        scratch_shapes=[
            pltpu.VMEM((NG, CELLS), BF16),
            pltpu.VMEM(constants.shape, BF16),
            pltpu.VMEM((3, SPREAD, 256), BF16),
            pltpu.VMEM((2, NG, CELLS), BF16),
            wide, wide, wide, wide,
            pltpu.VMEM((2, 4, 2, *slab), F32),
            pltpu.VMEM((2, 4, 2, *slab), F32),
            pltpu.VMEM(slab, F32),
            pltpu.VMEM(slab, F32),
            pltpu.VMEM((SLAB, 128), F32),
            dma((2,)),
            dma((2, CHUNKS)), dma((2, CHUNKS)),
            dma((2, 4, 2)), dma((2, 4, 2)),
            dma, dma,
            pltpu.SemaphoreType.REGULAR,
            pltpu.SemaphoreType.REGULAR((2,)),
        ],
        compiler_params=pltpu.CompilerParams(
            collective_id=0, has_side_effects=True, vmem_limit_bytes=54 * 2**20 - 2**17
        ),
    )(orbitals[0], constants)
    return found.transpose(1, 0, 2)


def solution(mesh):
    return jax.shard_map(
        on_device,
        mesh=mesh,
        in_specs=(P("blk", None, None),),
        out_specs=P("blk", "off", None),
        check_vma=False,
    )
```

```python
import math

import jax
import jax.numpy as jnp
import numpy as np
from jax import lax
from jax.experimental import pallas as pl
from jax.experimental.pallas import tpu as pltpu
from jax.sharding import PartitionSpec as P

MESH = pl.DeviceIdType.MESH
F32 = jnp.float32
BF16 = jnp.bfloat16

cell_edge = 59.0
screen_rate = 0.106

NG = 48
CELLS = NG * NG
HALF = 64
SLAB = 72
PACKED = 56
EARLY = 4
CHUNKS = 3
CHUNK = NG // CHUNKS


def tables():
    n = np.arange(NG)
    basis = np.zeros((NG, NG))
    basis[0] = 1.0 / math.sqrt(NG)
    for k in range(1, NG // 2):
        basis[k] = math.sqrt(2.0 / NG) * np.cos(2.0 * math.pi * ((k * n) % NG) / NG)
        basis[NG // 2 + k] = math.sqrt(2.0 / NG) * np.sin(2.0 * math.pi * ((k * n) % NG) / NG)
    basis[NG // 2] = np.cos(math.pi * n) / math.sqrt(NG)
    high = basis.astype(jnp.bfloat16).astype(np.float64)
    low = (basis - high).astype(jnp.bfloat16).astype(np.float64)

    def right(h, l):
        table = np.zeros((256, 256))
        for p in range(2):
            at = slice(p * HALF, p * HALF + NG)
            table[at, at] = h
            table[at, 128 + p * HALF : 128 + p * HALF + NG] = l
            table[128 + p * HALF : 128 + p * HALF + NG, at] = h
        return table

    def left(h, l):
        table = np.zeros((NG, 256))
        table[:, : 3 * NG] = np.concatenate([h, h, l], axis=1)
        return table

    whole = [right(high.T, low.T), right(high, low), left(high, low), left(high.T, low.T)]
    return np.concatenate(whole, axis=0).astype(jnp.bfloat16)


def halves(v):
    high = v.astype(BF16)
    low = (v - high.astype(F32)).astype(BF16)
    return high, low


def dot(a, b):
    return jnp.dot(a, b, preferred_element_type=F32)


def along_lanes(v, table):
    high, low = halves(v)
    both = dot(jnp.concatenate([high, low], axis=1), table)
    return both[:, :128] + both[:, 128:]


def along_rows(v, table):
    high, low = halves(v)
    return dot(table, jnp.concatenate([high, low, high], axis=0))


def to_lanes(v, count):
    return jnp.concatenate([v[i * NG : (i + 1) * NG] for i in range(count)], axis=1)


def to_rows(v, count):
    return jnp.concatenate([v[:, i * 128 : (i + 1) * 128] for i in range(count)], axis=0)


WINDOWS = ((0, 128, 0), (0, 256, 96), (128, 256, 64), (256, 128, 32))
STARTS = (0, 128, 384, 640)
SPREAD = 768


def fill_spread(spread_ref):
    for (_, depth, offset), start in zip(WINDOWS, STARTS):
        row = lax.broadcasted_iota(jnp.int32, (depth, 256), 0)
        lane = lax.broadcasted_iota(jnp.int32, (depth, 256), 1)
        cell = lane % HALF
        hit = (row == offset + NG * (lane // 128) + cell) & (cell < NG)
        second = (lane // HALF) % 2 == 1
        for which, kept in enumerate((hit & ~second, hit & second, hit)):
            spread_ref[which, start : start + depth, :] = jnp.where(kept, 1.0, 0.0).astype(BF16)


def spread(parts, spread_ref, out_ref, start, count):
    for pair, (first, depth, _) in enumerate(WINDOWS):
        total = None
        for ref, which in parts:
            rows = jnp.concatenate(
                [
                    ref[start : start + count, g * 384 + first : g * 384 + first + depth]
                    for g in range(6)
                ],
                axis=0,
            )
            term = dot(rows, spread_ref[which, STARTS[pair] : STARTS[pair] + depth, :])
            total = term if total is None else total + term
        for g in range(6):
            for side in range(2):
                y = g * 8 + pair * 2 + side
                out_ref[pl.ds(start * NG + y, count, stride=NG), :] = total[
                    g * count : (g + 1) * count, side * 128 : (side + 1) * 128
                ]


def gap_lanes(rows):
    return lax.broadcasted_iota(jnp.int32, (rows, 128), 1) % HALF >= NG


def packed(slab):
    moved = [
        pltpu.roll(slab[56 + 8 * (q // 3) : 64 + 8 * (q // 3)], NG - 16 * (q % 3), 1)
        for q in range(6)
    ]
    filled = jnp.where(gap_lanes(48), jnp.concatenate(moved, axis=0), slab[:48])
    return jnp.concatenate([filled, slab[48:56]], axis=0)


def unpacked(slab):
    place = lax.broadcasted_iota(jnp.int32, (8, 128), 1) % HALF // 16
    tiles = [slab]
    for v in range(2):
        tile = jnp.zeros((8, 128), F32)
        for q in range(3):
            piece = slab[(v * 3 + q) * 8 : (v * 3 + q) * 8 + 8]
            tile = jnp.where(place == q, pltpu.roll(piece, 80 + 16 * q, 1), tile)
        tiles.append(tile)
    return jnp.concatenate(tiles, axis=0)


def signed_square(k):
    m = jnp.where(k > NG // 2, k - NG // 2, k)
    return m * m


def fill_kernel(kernel_ref):
    row = lax.broadcasted_iota(jnp.int32, (NG, 128), 0)
    lane = lax.broadcasted_iota(jnp.int32, (NG, 128), 1) % HALF
    plane = signed_square(row) + signed_square(lane)

    def one(k, carry):
        squared = plane + signed_square(k)
        wave_sq = squared.astype(F32) * F32((2.0 * math.pi / cell_edge) ** 2)
        safe_sq = jnp.where(squared == 0, F32(1.0), wave_sq)
        damped = F32(1.0) - jnp.exp(-safe_sq * F32(1.0 / (4.0 * screen_rate**2)))
        screened = F32(4.0 * math.pi) * damped / safe_sq
        value = jnp.where(squared == 0, F32(math.pi / screen_rate**2), screened)
        kernel_ref[pl.ds(pl.multiple_of(k * NG, NG), NG), :] = value
        return carry

    lax.fori_loop(0, NG, one, 0)


def join_rows(planes_ref, out_ref):
    lane = lax.broadcasted_iota(jnp.int32, (3, 128), 1)
    full = [None] * (CELLS // 128)
    for y in range(NG):
        row = planes_ref[pl.ds(y % 24, 3, stride=24), :]
        tile, at = divmod(y * NG, 128)
        row = pltpu.roll(row, (at - HALF * (y // 24)) % 128, 1)
        full[tile] = row if at == 0 else jnp.where(lane < at, full[tile], row)
        if at + NG > 128:
            full[tile + 1] = row
    for tile, row in enumerate(full):
        for plane in range(3):
            out_ref[plane, :, tile * 128 : (tile + 1) * 128] = row[plane : plane + 1]


def pick(index, values):
    result = values[-1]
    for i in range(len(values) - 1):
        result = jnp.where(index == i, values[i], result)
    return result


def exchange_kernel(
    own_ref, table_ref, out_ref,
    own, table, spread_ref, partner, own_wide, partner_wide, field, kernel,
    partial, from_x, from_far, row_sum, from_y,
    planes_ref, copy_sem, in_send, in_recv, x_send, x_recv, y_send, y_recv, far_send, far_recv,
    opposite_sem, far_sem, go_sem,
):
    blk = lax.axis_index("blk")
    off = lax.axis_index("off")
    z, y_lo = blk // 4, blk % 4
    x, y_hi, core = off // 4, (off // 2) % 2, off % 2
    y = y_hi * 4 + y_lo

    load_own = pltpu.make_async_copy(own_ref, own, copy_sem.at[0])
    load_table = pltpu.make_async_copy(table_ref, table, copy_sem.at[1])
    load_own.start()
    load_table.start()

    def device(x, y, z, core):
        y = lax.rem(y + 8, 8)
        z = lax.rem(z + 8, 8)
        return (z * 4 + lax.rem(y, 4), (x * 2 + y // 4) * 2 + core)

    sources, targets = [], []
    for k in range(2):
        dy = pick(lax.rem(core * 2 + k + x, 4), (0, 1, 2 - 4 * lax.rem(y, 2), -1))

        def dz_of(y_hi):
            even = jnp.where(core == 0, 4 * k, 2 - 4 * k)
            odd = jnp.where(core == 0, 1 - 4 * k, 3 - 4 * k)
            return jnp.where(y_hi == 0, even, odd)

        sources.append(device(x, y + dy, z + dz_of(y_hi), core))
        ty = lax.rem(y - dy + 8, 8)
        targets.append(device(x, ty, z - dz_of(ty // 4), core))
    itself = (x == 0) & (y_hi == 0) & (core == 0)
    opposite = (blk, (x * 2 + 1 - y_hi) * 2 + core)

    def neighbour(ahead, other):
        cx = lax.rem(x + ahead, 4)
        return (blk, (cx * 2 + y_hi) * 2 + (1 - core if other else core))

    around = [(ahead, other) for ahead in (1, 2, 3, 0) for other in range(2) if ahead or other]

    barrier = pltpu.get_barrier_semaphore()

    def greet(device_id):
        pl.semaphore_signal(barrier, inc=1, device_id=device_id, device_id_type=MESH)

    below, above = device(x, y - 2, z, core), device(x, y + 2, z, core)
    greet(below)
    greet(above)
    for ahead, other in around:
        greet(neighbour(ahead, other))

    mine_early = z < EARLY
    moves = (jnp.logical_not(itself), itself | True)
    to_early = [target[0] // 4 < EARLY for target in targets]
    from_early = [source[0] // 4 < EARLY for source in sources]
    defer_to = [moves[k] & mine_early & jnp.logical_not(to_early[k]) for k in range(2)]
    defer_from = [moves[k] & jnp.logical_not(mine_early) & from_early[k] for k in range(2)]
    greetings = 9
    for k in range(2):

        @pl.when(moves[k] & jnp.logical_not(defer_from[k]))
        def _():
            greet(sources[k])

        @pl.when(defer_to[k])
        def _():
            greet(targets[k])

        greetings = greetings + jnp.where(moves[k] & jnp.logical_not(defer_to[k]), 1, 0)
        greetings = greetings + jnp.where(defer_from[k], 1, 0)

    pl.semaphore_wait(barrier, greetings)

    for k in range(2):

        @pl.when(defer_from[k])
        def _():
            pl.semaphore_signal(
                go_sem.at[k], inc=1, device_id=sources[k], device_id_type=MESH
            )

    def arrival(k, c):
        at = pl.ds(c * CHUNK, CHUNK)
        return pltpu.make_async_remote_copy(
            src_ref=own_ref.at[at],
            dst_ref=partner.at[k, at],
            send_sem=in_send.at[k, c],
            recv_sem=in_recv.at[k, c],
            device_id=targets[k],
            device_id_type=MESH,
        )

    later = [
        moves[k] & jnp.logical_not(mine_early | to_early[k]) & to_early[1 - k]
        for k in range(2)
    ]
    for c in range(CHUNKS):
        for k in range(2):

            @pl.when(moves[k] & jnp.logical_not(defer_to[k] | later[k]))
            def _():
                arrival(k, c).start()

    pl.semaphore_signal(opposite_sem, inc=1, device_id=below, device_id_type=MESH)
    fill_spread(spread_ref)
    load_own.wait()
    spread([(own, 2)], spread_ref, own_wide, 0, NG)
    fill_kernel(kernel)
    load_table.wait()

    pl.semaphore_wait(opposite_sem, 1)
    for other in range(2):
        pl.semaphore_signal(
            far_sem, inc=1, device_id=neighbour(2, other), device_id_type=MESH
        )

    for k in range(2):

        @pl.when(defer_to[k])
        def _():
            pl.semaphore_wait(go_sem.at[k], 1)
            for c in range(CHUNKS):
                arrival(k, c).start()

        @pl.when(later[k])
        def _():
            for c in range(CHUNKS):
                arrival(1 - k, c).wait_send()
            for c in range(CHUNKS):
                arrival(k, c).start()

    right_forward = table.at[pl.ds(0, 256)]
    right_backward = table.at[pl.ds(256, 256)]
    left_forward = table.at[pl.ds(512, NG), pl.ds(0, 3 * NG)]
    left_backward = table.at[pl.ds(512 + NG, NG), pl.ds(0, 3 * NG)]

    @pl.when(itself)
    def _():
        partner[0] = own[...]

    for c in range(CHUNKS):

        @pl.when(moves[0])
        def _():
            arrival(0, c).wait_recv()

        arrival(1, c).wait_recv()
        spread([(partner.at[0], 0), (partner.at[1], 1)], spread_ref, partner_wide, c * CHUNK, CHUNK)
        at = pl.ds(c * CHUNK * NG, CHUNK * NG)
        density = own_wide[at, :] * partner_wide[at, :]
        wide = to_lanes(along_lanes(density, right_forward[...]), CHUNK)
        field[at, :] = to_rows(along_rows(wide, left_forward[...]), CHUNK)

    columns = [field[pl.ds(j, NG, stride=NG), :] for j in range(NG)]
    spectrum = along_rows(jnp.concatenate(columns, axis=1), left_forward[...])
    back = along_rows(spectrum * to_lanes(kernel[...], NG), left_backward[...])
    for j in range(NG):
        field[pl.ds(j, NG, stride=NG), :] = back[:, j * 128 : (j + 1) * 128]

    def departure(h, ahead, other):
        return pltpu.make_async_remote_copy(
            src_ref=partial.at[h, ahead, other],
            dst_ref=from_x.at[h, (4 - ahead) % 4, other],
            send_sem=x_send.at[h, ahead, other],
            recv_sem=x_recv.at[h, (4 - ahead) % 4, other],
            device_id=neighbour(ahead, other),
            device_id_type=MESH,
        )

    def straight(other):
        cx = lax.rem(x + 2, 4)
        return pltpu.make_async_remote_copy(
            src_ref=partial.at[0, 2, other],
            dst_ref=from_far.at[other],
            send_sem=far_send.at[other],
            recv_sem=far_recv.at[other],
            device_id=(blk, (cx * 2 + 1 - y_hi) * 2 + (1 - core if other else core)),
            device_id_type=MESH,
        )

    low_half = lax.broadcasted_iota(jnp.int32, (NG // 2, 128), 1) < HALF

    def slabs(h):
        kept_hi = 1 - y_hi if h == 0 else y_hi
        starts = [
            pl.multiple_of((lax.rem(x + ahead, 4) * 2 + kept_hi) * (6 * NG), 6 * NG)
            for ahead in range(4)
        ]
        spectrum = jnp.concatenate([field[pl.ds(at, 6 * NG), :] for at in starts], axis=0)
        wide = along_rows(to_lanes(spectrum, 24), left_backward[...])
        potential = along_lanes(to_rows(wide, 24), right_backward[...])
        for ahead in (2, 1, 3, 0):
            terms = (
                potential[ahead * 6 * NG : (ahead + 1) * 6 * NG]
                * partner_wide[pl.ds(starts[ahead], 6 * NG), :]
            )
            for side in range(2):
                planes = []
                for i in range(side * 3, side * 3 + 3):
                    a = terms[i * NG : i * NG + NG // 2]
                    b = terms[i * NG + NG // 2 : (i + 1) * NG]
                    swapped = pltpu.roll(jnp.where(low_half, b, a), HALF, 1)
                    planes.append(jnp.where(low_half, a, b) + swapped)
                other = jnp.where(core == side, 0, 1)
                partial[h, ahead, other] = packed(jnp.concatenate(planes, axis=0))
            for other in range(2):
                if h == 0 and ahead == 2:
                    straight(other).start()
                elif ahead or other:
                    departure(h, ahead, other).start()

    pl.semaphore_wait(far_sem, 2)
    slabs(0)
    slabs(1)

    def gathered(h):
        total = partial[h, 0, 0]
        near = [(ahead, other) for ahead, other in around if h or ahead != 2]
        for ahead, other in near:
            departure(h, ahead, other).wait()
        for ahead, other in near:
            total = total + from_x[h, ahead, other]
        return total

    row_sum[...] = gathered(0)
    last = pltpu.make_async_remote_copy(
        src_ref=row_sum,
        dst_ref=from_y,
        send_sem=y_send,
        recv_sem=y_recv,
        device_id=opposite,
        device_id_type=MESH,
    )
    last.start()
    kept = gathered(1)
    for other in range(2):
        straight(other).wait()
    kept = kept + (from_far[0] + from_far[1])

    for k in range(2):

        @pl.when(moves[k] & jnp.logical_not(later[1 - k]))
        def _():
            for c in range(CHUNKS):
                arrival(k, c).wait_send()

    last.wait()
    planes_ref[...] = unpacked(F32(-0.25) * (kept + from_y[...]))
    join_rows(planes_ref, out_ref)


def on_device(orbitals):
    anywhere = pl.BlockSpec(memory_space=pl.ANY)
    wide = pltpu.VMEM((CELLS, 128), F32)
    slab = (PACKED, 128)
    dma = pltpu.SemaphoreType.DMA
    constants = jnp.asarray(tables())
    found = pl.pallas_call(
        exchange_kernel,
        out_shape=jax.ShapeDtypeStruct((3, 1, CELLS), F32),
        in_specs=[anywhere, anywhere],
        out_specs=pl.BlockSpec(memory_space=pltpu.VMEM),
        scratch_shapes=[
            pltpu.VMEM((NG, CELLS), BF16),
            pltpu.VMEM(constants.shape, BF16),
            pltpu.VMEM((3, SPREAD, 256), BF16),
            pltpu.VMEM((2, NG, CELLS), BF16),
            wide, wide, wide, wide,
            pltpu.VMEM((2, 4, 2, *slab), F32),
            pltpu.VMEM((2, 4, 2, *slab), F32),
            pltpu.VMEM((2, *slab), F32),
            pltpu.VMEM(slab, F32),
            pltpu.VMEM(slab, F32),
            pltpu.VMEM((SLAB, 128), F32),
            dma((2,)),
            dma((2, CHUNKS)), dma((2, CHUNKS)),
            dma((2, 4, 2)), dma((2, 4, 2)),
            dma, dma,
            dma((2,)), dma((2,)),
            pltpu.SemaphoreType.REGULAR,
            pltpu.SemaphoreType.REGULAR,
            pltpu.SemaphoreType.REGULAR((2,)),
        ],
        compiler_params=pltpu.CompilerParams(
            collective_id=0, has_side_effects=True, vmem_limit_bytes=54 * 2**20 - 2**17
        ),
    )(orbitals[0], constants)
    return found.transpose(1, 0, 2)


def solution(mesh):
    return jax.shard_map(
        on_device,
        mesh=mesh,
        in_specs=(P("blk", None, None),),
        out_specs=P("blk", "off", None),
        check_vma=False,
    )
```

```python
import math

import jax
import jax.numpy as jnp
import numpy as np
from jax import lax
from jax.experimental import pallas as pl
from jax.experimental.pallas import tpu as pltpu
from jax.sharding import PartitionSpec as P

MESH = pl.DeviceIdType.MESH
F32 = jnp.float32
BF16 = jnp.bfloat16

cell_edge = 59.0
screen_rate = 0.106

NG = 48
CELLS = NG * NG
HALF = 64
SLAB = 72
PACKED = 56
EARLY = 3
CHUNKS = 3
CHUNK = NG // CHUNKS


def tables():
    n = np.arange(NG)
    basis = np.zeros((NG, NG))
    basis[0] = 1.0 / math.sqrt(NG)
    for k in range(1, NG // 2):
        basis[k] = math.sqrt(2.0 / NG) * np.cos(2.0 * math.pi * ((k * n) % NG) / NG)
        basis[NG // 2 + k] = math.sqrt(2.0 / NG) * np.sin(2.0 * math.pi * ((k * n) % NG) / NG)
    basis[NG // 2] = np.cos(math.pi * n) / math.sqrt(NG)
    high = basis.astype(jnp.bfloat16).astype(np.float64)
    low = (basis - high).astype(jnp.bfloat16).astype(np.float64)

    def right(h, l):
        table = np.zeros((256, 256))
        for p in range(2):
            at = slice(p * HALF, p * HALF + NG)
            table[at, at] = h
            table[at, 128 + p * HALF : 128 + p * HALF + NG] = l
            table[128 + p * HALF : 128 + p * HALF + NG, at] = h
        return table

    def left(h, l):
        table = np.zeros((NG, 256))
        table[:, : 3 * NG] = np.concatenate([h, h, l], axis=1)
        return table

    whole = [right(high.T, low.T), right(high, low), left(high, low), left(high.T, low.T)]
    return np.concatenate(whole, axis=0).astype(jnp.bfloat16)


def halves(v):
    high = v.astype(BF16)
    low = (v - high.astype(F32)).astype(BF16)
    return high, low


def dot(a, b):
    return jnp.dot(a, b, preferred_element_type=F32)


def along_lanes(v, table):
    high, low = halves(v)
    both = dot(jnp.concatenate([high, low], axis=1), table)
    return both[:, :128] + both[:, 128:]


def along_rows(v, table):
    high, low = halves(v)
    return dot(table, jnp.concatenate([high, low, high], axis=0))


def to_lanes(v, count):
    return jnp.concatenate([v[i * NG : (i + 1) * NG] for i in range(count)], axis=1)


def to_rows(v, count):
    return jnp.concatenate([v[:, i * 128 : (i + 1) * 128] for i in range(count)], axis=0)


WINDOWS = ((0, 128, 0), (0, 256, 96), (128, 256, 64), (256, 128, 32))
STARTS = (0, 128, 384, 640)
SPREAD = 768


def fill_spread(spread_ref):
    for (_, depth, offset), start in zip(WINDOWS, STARTS):
        row = lax.broadcasted_iota(jnp.int32, (depth, 256), 0)
        lane = lax.broadcasted_iota(jnp.int32, (depth, 256), 1)
        cell = lane % HALF
        hit = (row == offset + NG * (lane // 128) + cell) & (cell < NG)
        second = (lane // HALF) % 2 == 1
        for which, kept in enumerate((hit & ~second, hit & second, hit)):
            spread_ref[which, start : start + depth, :] = jnp.where(kept, 1.0, 0.0).astype(BF16)


def spread(parts, spread_ref, out_ref, start, count):
    for pair, (first, depth, _) in enumerate(WINDOWS):
        total = None
        for ref, which in parts:
            rows = jnp.concatenate(
                [
                    ref[start : start + count, g * 384 + first : g * 384 + first + depth]
                    for g in range(6)
                ],
                axis=0,
            )
            term = dot(rows, spread_ref[which, STARTS[pair] : STARTS[pair] + depth, :])
            total = term if total is None else total + term
        for g in range(6):
            for side in range(2):
                y = g * 8 + pair * 2 + side
                out_ref[pl.ds(start * NG + y, count, stride=NG), :] = total[
                    g * count : (g + 1) * count, side * 128 : (side + 1) * 128
                ]


def gap_lanes(rows):
    return lax.broadcasted_iota(jnp.int32, (rows, 128), 1) % HALF >= NG


def packed(slab):
    moved = [
        pltpu.roll(slab[56 + 8 * (q // 3) : 64 + 8 * (q // 3)], NG - 16 * (q % 3), 1)
        for q in range(6)
    ]
    filled = jnp.where(gap_lanes(48), jnp.concatenate(moved, axis=0), slab[:48])
    return jnp.concatenate([filled, slab[48:56]], axis=0)


def unpacked(slab):
    place = lax.broadcasted_iota(jnp.int32, (8, 128), 1) % HALF // 16
    tiles = [slab]
    for v in range(2):
        tile = jnp.zeros((8, 128), F32)
        for q in range(3):
            piece = slab[(v * 3 + q) * 8 : (v * 3 + q) * 8 + 8]
            tile = jnp.where(place == q, pltpu.roll(piece, 80 + 16 * q, 1), tile)
        tiles.append(tile)
    return jnp.concatenate(tiles, axis=0)


def signed_square(k):
    m = jnp.where(k > NG // 2, k - NG // 2, k)
    return m * m


def fill_kernel(kernel_ref):
    row = lax.broadcasted_iota(jnp.int32, (NG, 128), 0)
    lane = lax.broadcasted_iota(jnp.int32, (NG, 128), 1) % HALF
    plane = signed_square(row) + signed_square(lane)

    def one(k, carry):
        squared = plane + signed_square(k)
        wave_sq = squared.astype(F32) * F32((2.0 * math.pi / cell_edge) ** 2)
        safe_sq = jnp.where(squared == 0, F32(1.0), wave_sq)
        damped = F32(1.0) - jnp.exp(-safe_sq * F32(1.0 / (4.0 * screen_rate**2)))
        screened = F32(4.0 * math.pi) * damped / safe_sq
        value = jnp.where(squared == 0, F32(math.pi / screen_rate**2), screened)
        kernel_ref[pl.ds(pl.multiple_of(k * NG, NG), NG), :] = value
        return carry

    lax.fori_loop(0, NG, one, 0)


def join_rows(planes_ref, out_ref):
    lane = lax.broadcasted_iota(jnp.int32, (3, 128), 1)
    full = [None] * (CELLS // 128)
    for y in range(NG):
        row = planes_ref[pl.ds(y % 24, 3, stride=24), :]
        tile, at = divmod(y * NG, 128)
        row = pltpu.roll(row, (at - HALF * (y // 24)) % 128, 1)
        full[tile] = row if at == 0 else jnp.where(lane < at, full[tile], row)
        if at + NG > 128:
            full[tile + 1] = row
    for tile, row in enumerate(full):
        for plane in range(3):
            out_ref[plane, :, tile * 128 : (tile + 1) * 128] = row[plane : plane + 1]


def pick(index, values):
    result = values[-1]
    for i in range(len(values) - 1):
        result = jnp.where(index == i, values[i], result)
    return result


def exchange_kernel(
    own_ref, table_ref, out_ref,
    own, table, spread_ref, partner, own_wide, partner_wide, field, kernel,
    partial, from_x, from_far, row_sum, from_y,
    planes_ref, copy_sem, in_send, in_recv, x_send, x_recv, y_send, y_recv, far_send, far_recv,
    opposite_sem, far_sem, go_sem,
):
    blk = lax.axis_index("blk")
    off = lax.axis_index("off")
    z, y_lo = blk // 4, blk % 4
    x, y_hi, core = off // 4, (off // 2) % 2, off % 2
    y = y_hi * 4 + y_lo

    load_own = pltpu.make_async_copy(own_ref, own, copy_sem.at[0])
    load_table = pltpu.make_async_copy(table_ref, table, copy_sem.at[1])
    load_own.start()
    load_table.start()

    def device(x, y, z, core):
        y = lax.rem(y + 8, 8)
        z = lax.rem(z + 8, 8)
        return (z * 4 + lax.rem(y, 4), (x * 2 + y // 4) * 2 + core)

    aside = jnp.where(core == 0, 0, 2 * lax.rem(y, 2) - 1)
    sign = 1 - 2 * lax.rem(z, 2)

    def dz_of(y_hi):
        even = jnp.where(core == 0, pick(x, (2, -2, 0, 4)), pick(x, (-2, 2, 4, 0)))
        odd = jnp.where(core == 0, pick(x, (3, -3, 1, -1)), pick(x, (-1, 1, -3, 3)))
        return jnp.where(y_hi == 1, even, odd * sign)

    there = lax.rem(y + aside + 8, 8)
    source = device(x, there, z + dz_of(y_hi), core)
    dz_there = dz_of(there // 4)
    target = device(x, there, jnp.where(there // 4 == 1, z - dz_there, z + dz_there), core)
    mate_y = y + 1 - 2 * lax.rem(y, 2)
    mate = device(x, mate_y, z, core)
    mate_source = device(x, mate_y - aside, z + dz_of(y_hi), core)
    target_z = lax.rem(target[0] // 4, 8)
    target_mate = device(x, there + 1 - 2 * lax.rem(there, 2), target_z, core)
    itself = (x == 2) & (y_hi == 1) & (core == 0)
    opposite = (blk, (x * 2 + 1 - y_hi) * 2 + core)

    def neighbour(ahead, other):
        cx = lax.rem(x + ahead, 4)
        return (blk, (cx * 2 + y_hi) * 2 + (1 - core if other else core))

    around = [(ahead, other) for ahead in (1, 2, 3, 0) for other in range(2) if ahead or other]

    barrier = pltpu.get_barrier_semaphore()

    def greet(device_id):
        pl.semaphore_signal(barrier, inc=1, device_id=device_id, device_id_type=MESH)

    below, above = device(x, y - 2, z, core), device(x, y + 2, z, core)
    greet(below)
    greet(above)
    for ahead, other in around:
        greet(neighbour(ahead, other))

    moves = jnp.logical_not(itself)
    early = z < EARLY
    defer_to = moves & early & (target[0] // 4 >= EARLY)
    defer_from = moves & jnp.logical_not(early) & (source[0] // 4 < EARLY)
    double_out = moves & jnp.logical_not(early) & (target_z < EARLY)
    double_in = moves & early & (source[0] // 4 >= EARLY)
    greet(mate)

    @pl.when(double_in)
    def _():
        greet(mate_source)

    @pl.when(moves & jnp.logical_not(defer_from))
    def _():
        greet(source)

    @pl.when(defer_to)
    def _():
        greet(target)

    pl.semaphore_wait(
        barrier,
        10
        + jnp.where(moves & jnp.logical_not(defer_to), 1, 0)
        + jnp.where(defer_from, 1, 0)
        + jnp.where(double_out, 1, 0),
    )

    @pl.when(defer_from)
    def _():
        pl.semaphore_signal(go_sem, inc=1, device_id=source, device_id_type=MESH)

    def arrival(k, c):
        at = pl.ds(c * CHUNK, CHUNK)
        slot = min(k, 1)
        return pltpu.make_async_remote_copy(
            src_ref=partner.at[0, at] if k == 1 else own_ref.at[at],
            dst_ref=partner.at[slot, at],
            send_sem=in_send.at[k, c],
            recv_sem=in_recv.at[slot, c],
            device_id=(target, mate, target_mate)[k],
            device_id_type=MESH,
        )

    for c in range(CHUNKS):

        @pl.when(moves & jnp.logical_not(defer_to))
        def _():
            arrival(0, c).start()

        @pl.when(double_out)
        def _():
            arrival(2, c).start()

    pl.semaphore_signal(opposite_sem, inc=1, device_id=below, device_id_type=MESH)
    fill_spread(spread_ref)
    load_own.wait()
    spread([(own, 2)], spread_ref, own_wide, 0, NG)
    fill_kernel(kernel)
    load_table.wait()

    pl.semaphore_wait(opposite_sem, 1)
    for other in range(2):
        pl.semaphore_signal(
            far_sem, inc=1, device_id=neighbour(2, other), device_id_type=MESH
        )

    @pl.when(defer_to)
    def _():
        pl.semaphore_wait(go_sem, 1)
        for c in range(CHUNKS):
            arrival(0, c).start()

    right_forward = table.at[pl.ds(0, 256)]
    right_backward = table.at[pl.ds(256, 256)]
    left_forward = table.at[pl.ds(512, NG), pl.ds(0, 3 * NG)]
    left_backward = table.at[pl.ds(512 + NG, NG), pl.ds(0, 3 * NG)]

    @pl.when(itself)
    def _():
        partner[0] = own[...]

    def pass_on(c):
        @pl.when(moves)
        def _():
            arrival(0, c).wait_recv()

        @pl.when(jnp.logical_not(double_in))
        def _():
            arrival(1, c).start()

    pass_on(0)
    for c in range(CHUNKS):
        if c + 1 < CHUNKS:
            pass_on(c + 1)
        arrival(1, c).wait_recv()
        spread([(partner.at[0], 0), (partner.at[1], 1)], spread_ref, partner_wide, c * CHUNK, CHUNK)
        at = pl.ds(c * CHUNK * NG, CHUNK * NG)
        density = own_wide[at, :] * partner_wide[at, :]
        wide = to_lanes(along_lanes(density, right_forward[...]), CHUNK)
        field[at, :] = to_rows(along_rows(wide, left_forward[...]), CHUNK)

    columns = [field[pl.ds(j, NG, stride=NG), :] for j in range(NG)]
    spectrum = along_rows(jnp.concatenate(columns, axis=1), left_forward[...])
    back = along_rows(spectrum * to_lanes(kernel[...], NG), left_backward[...])
    for j in range(NG):
        field[pl.ds(j, NG, stride=NG), :] = back[:, j * 128 : (j + 1) * 128]

    def departure(h, ahead, other):
        return pltpu.make_async_remote_copy(
            src_ref=partial.at[h, ahead, other],
            dst_ref=from_x.at[h, (4 - ahead) % 4, other],
            send_sem=x_send.at[h, ahead, other],
            recv_sem=x_recv.at[h, (4 - ahead) % 4, other],
            device_id=neighbour(ahead, other),
            device_id_type=MESH,
        )

    def straight(other):
        cx = lax.rem(x + 2, 4)
        return pltpu.make_async_remote_copy(
            src_ref=partial.at[0, 2, other],
            dst_ref=from_far.at[other],
            send_sem=far_send.at[other],
            recv_sem=far_recv.at[other],
            device_id=(blk, (cx * 2 + 1 - y_hi) * 2 + (1 - core if other else core)),
            device_id_type=MESH,
        )

    low_half = lax.broadcasted_iota(jnp.int32, (NG // 2, 128), 1) < HALF

    def slabs(h):
        kept_hi = 1 - y_hi if h == 0 else y_hi
        starts = [
            pl.multiple_of((lax.rem(x + ahead, 4) * 2 + kept_hi) * (6 * NG), 6 * NG)
            for ahead in range(4)
        ]
        spectrum = jnp.concatenate([field[pl.ds(at, 6 * NG), :] for at in starts], axis=0)
        wide = along_rows(to_lanes(spectrum, 24), left_backward[...])
        potential = along_lanes(to_rows(wide, 24), right_backward[...])
        for ahead in (2, 1, 3, 0):
            terms = (
                potential[ahead * 6 * NG : (ahead + 1) * 6 * NG]
                * partner_wide[pl.ds(starts[ahead], 6 * NG), :]
            )
            for side in range(2):
                planes = []
                for i in range(side * 3, side * 3 + 3):
                    a = terms[i * NG : i * NG + NG // 2]
                    b = terms[i * NG + NG // 2 : (i + 1) * NG]
                    swapped = pltpu.roll(jnp.where(low_half, b, a), HALF, 1)
                    planes.append(jnp.where(low_half, a, b) + swapped)
                other = jnp.where(core == side, 0, 1)
                partial[h, ahead, other] = packed(jnp.concatenate(planes, axis=0))
            for other in range(2):
                if h == 0 and ahead == 2:
                    straight(other).start()
                elif ahead or other:
                    departure(h, ahead, other).start()

    pl.semaphore_wait(far_sem, 2)
    slabs(0)
    slabs(1)

    def gathered(h):
        total = partial[h, 0, 0]
        near = [(ahead, other) for ahead, other in around if h or ahead != 2]
        for ahead, other in near:
            departure(h, ahead, other).wait()
        for ahead, other in near:
            total = total + from_x[h, ahead, other]
        return total

    row_sum[...] = gathered(0)
    last = pltpu.make_async_remote_copy(
        src_ref=row_sum,
        dst_ref=from_y,
        send_sem=y_send,
        recv_sem=y_recv,
        device_id=opposite,
        device_id_type=MESH,
    )
    last.start()
    kept = gathered(1)
    for other in range(2):
        straight(other).wait()
    kept = kept + (from_far[0] + from_far[1])

    for c in range(CHUNKS):

        @pl.when(moves)
        def _():
            arrival(0, c).wait_send()

        @pl.when(jnp.logical_not(double_in))
        def _():
            arrival(1, c).wait_send()

        @pl.when(double_out)
        def _():
            arrival(2, c).wait_send()

    last.wait()
    planes_ref[...] = unpacked(F32(-0.25) * (kept + from_y[...]))
    join_rows(planes_ref, out_ref)


def on_device(orbitals):
    anywhere = pl.BlockSpec(memory_space=pl.ANY)
    wide = pltpu.VMEM((CELLS, 128), F32)
    slab = (PACKED, 128)
    dma = pltpu.SemaphoreType.DMA
    constants = jnp.asarray(tables())
    found = pl.pallas_call(
        exchange_kernel,
        out_shape=jax.ShapeDtypeStruct((3, 1, CELLS), F32),
        in_specs=[anywhere, anywhere],
        out_specs=pl.BlockSpec(memory_space=pltpu.VMEM),
        scratch_shapes=[
            pltpu.VMEM((NG, CELLS), BF16),
            pltpu.VMEM(constants.shape, BF16),
            pltpu.VMEM((3, SPREAD, 256), BF16),
            pltpu.VMEM((2, NG, CELLS), BF16),
            wide, wide, wide, wide,
            pltpu.VMEM((2, 4, 2, *slab), F32),
            pltpu.VMEM((2, 4, 2, *slab), F32),
            pltpu.VMEM((2, *slab), F32),
            pltpu.VMEM(slab, F32),
            pltpu.VMEM(slab, F32),
            pltpu.VMEM((SLAB, 128), F32),
            dma((2,)),
            dma((3, CHUNKS)), dma((2, CHUNKS)),
            dma((2, 4, 2)), dma((2, 4, 2)),
            dma, dma,
            dma((2,)), dma((2,)),
            pltpu.SemaphoreType.REGULAR,
            pltpu.SemaphoreType.REGULAR,
            pltpu.SemaphoreType.REGULAR,
        ],
        compiler_params=pltpu.CompilerParams(
            collective_id=0, has_side_effects=True, vmem_limit_bytes=54 * 2**20 - 2**17
        ),
    )(orbitals[0], constants)
    return found.transpose(1, 0, 2)


def solution(mesh):
    return jax.shard_map(
        on_device,
        mesh=mesh,
        in_specs=(P("blk", None, None),),
        out_specs=P("blk", "off", None),
        check_vma=False,
    )
```

```python
import math

import jax
import jax.numpy as jnp
import numpy as np
from jax import lax
from jax.experimental import pallas as pl
from jax.experimental.pallas import tpu as pltpu
from jax.sharding import PartitionSpec as P

MESH = pl.DeviceIdType.MESH
F32 = jnp.float32
BF16 = jnp.bfloat16

cell_edge = 59.0
screen_rate = 0.106

NG = 48
CELLS = NG * NG
HALF = 64
SLAB = 72
PACKED = 56
EARLY = 3
CHUNKS = 3
CHUNK = NG // CHUNKS


def tables():
    n = np.arange(NG)
    basis = np.zeros((NG, NG))
    basis[0] = 1.0 / math.sqrt(NG)
    for k in range(1, NG // 2):
        basis[k] = math.sqrt(2.0 / NG) * np.cos(2.0 * math.pi * ((k * n) % NG) / NG)
        basis[NG // 2 + k] = math.sqrt(2.0 / NG) * np.sin(2.0 * math.pi * ((k * n) % NG) / NG)
    basis[NG // 2] = np.cos(math.pi * n) / math.sqrt(NG)
    high = basis.astype(jnp.bfloat16).astype(np.float64)
    low = (basis - high).astype(jnp.bfloat16).astype(np.float64)

    def right(h, l):
        table = np.zeros((256, 256))
        for p in range(2):
            at = slice(p * HALF, p * HALF + NG)
            table[at, at] = h
            table[at, 128 + p * HALF : 128 + p * HALF + NG] = l
            table[128 + p * HALF : 128 + p * HALF + NG, at] = h
        return table

    def left(h, l):
        table = np.zeros((NG, 256))
        table[:, : 3 * NG] = np.concatenate([h, h, l], axis=1)
        return table

    whole = [right(high.T, low.T), right(high, low), left(high, low), left(high.T, low.T)]
    return np.concatenate(whole, axis=0).astype(jnp.bfloat16)


def halves(v):
    high = v.astype(BF16)
    low = (v - high.astype(F32)).astype(BF16)
    return high, low


def dot(a, b):
    return jnp.dot(a, b, preferred_element_type=F32)


def along_lanes(v, table):
    high, low = halves(v)
    both = dot(jnp.concatenate([high, low], axis=1), table)
    return both[:, :128] + both[:, 128:]


def along_rows(v, table):
    high, low = halves(v)
    return dot(table, jnp.concatenate([high, low, high], axis=0))


def to_lanes(v, count):
    return jnp.concatenate([v[i * NG : (i + 1) * NG] for i in range(count)], axis=1)


def to_rows(v, count):
    return jnp.concatenate([v[:, i * 128 : (i + 1) * 128] for i in range(count)], axis=0)


WINDOWS = ((0, 128, 0), (0, 256, 96), (128, 256, 64), (256, 128, 32))
STARTS = (0, 128, 384, 640)
SPREAD = 768


def fill_spread(spread_ref):
    for (_, depth, offset), start in zip(WINDOWS, STARTS):
        row = lax.broadcasted_iota(jnp.int32, (depth, 256), 0)
        lane = lax.broadcasted_iota(jnp.int32, (depth, 256), 1)
        cell = lane % HALF
        hit = (row == offset + NG * (lane // 128) + cell) & (cell < NG)
        second = (lane // HALF) % 2 == 1
        for which, kept in enumerate((hit & ~second, hit & second, hit)):
            spread_ref[which, start : start + depth, :] = jnp.where(kept, 1.0, 0.0).astype(BF16)


def spread(parts, spread_ref, out_ref, start, count):
    for pair, (first, depth, _) in enumerate(WINDOWS):
        total = None
        for ref, which in parts:
            rows = jnp.concatenate(
                [
                    ref[start : start + count, g * 384 + first : g * 384 + first + depth]
                    for g in range(6)
                ],
                axis=0,
            )
            term = dot(rows, spread_ref[which, STARTS[pair] : STARTS[pair] + depth, :])
            total = term if total is None else total + term
        for g in range(6):
            for side in range(2):
                y = g * 8 + pair * 2 + side
                out_ref[pl.ds(start * NG + y, count, stride=NG), :] = total[
                    g * count : (g + 1) * count, side * 128 : (side + 1) * 128
                ]


def gap_lanes(rows):
    return lax.broadcasted_iota(jnp.int32, (rows, 128), 1) % HALF >= NG


def packed(slab):
    moved = [
        pltpu.roll(slab[56 + 8 * (q // 3) : 64 + 8 * (q // 3)], NG - 16 * (q % 3), 1)
        for q in range(6)
    ]
    filled = jnp.where(gap_lanes(48), jnp.concatenate(moved, axis=0), slab[:48])
    return jnp.concatenate([filled, slab[48:56]], axis=0)


def unpacked(slab):
    place = lax.broadcasted_iota(jnp.int32, (8, 128), 1) % HALF // 16
    tiles = [slab]
    for v in range(2):
        tile = jnp.zeros((8, 128), F32)
        for q in range(3):
            piece = slab[(v * 3 + q) * 8 : (v * 3 + q) * 8 + 8]
            tile = jnp.where(place == q, pltpu.roll(piece, 80 + 16 * q, 1), tile)
        tiles.append(tile)
    return jnp.concatenate(tiles, axis=0)


def signed_square(k):
    m = jnp.where(k > NG // 2, k - NG // 2, k)
    return m * m


def fill_kernel(kernel_ref):
    row = lax.broadcasted_iota(jnp.int32, (NG, 128), 0)
    lane = lax.broadcasted_iota(jnp.int32, (NG, 128), 1) % HALF
    plane = signed_square(row) + signed_square(lane)

    def one(k, carry):
        squared = plane + signed_square(k)
        wave_sq = squared.astype(F32) * F32((2.0 * math.pi / cell_edge) ** 2)
        safe_sq = jnp.where(squared == 0, F32(1.0), wave_sq)
        damped = F32(1.0) - jnp.exp(-safe_sq * F32(1.0 / (4.0 * screen_rate**2)))
        screened = F32(4.0 * math.pi) * damped / safe_sq
        value = jnp.where(squared == 0, F32(math.pi / screen_rate**2), screened)
        kernel_ref[pl.ds(pl.multiple_of(k * NG, NG), NG), :] = value
        return carry

    lax.fori_loop(0, NG, one, 0)


def join_rows(planes_ref, out_ref):
    lane = lax.broadcasted_iota(jnp.int32, (3, 128), 1)
    full = [None] * (CELLS // 128)
    for y in range(NG):
        row = planes_ref[pl.ds(y % 24, 3, stride=24), :]
        tile, at = divmod(y * NG, 128)
        row = pltpu.roll(row, (at - HALF * (y // 24)) % 128, 1)
        full[tile] = row if at == 0 else jnp.where(lane < at, full[tile], row)
        if at + NG > 128:
            full[tile + 1] = row
    for tile, row in enumerate(full):
        for plane in range(3):
            out_ref[plane, :, tile * 128 : (tile + 1) * 128] = row[plane : plane + 1]


def pick(index, values):
    result = values[-1]
    for i in range(len(values) - 1):
        result = jnp.where(index == i, values[i], result)
    return result


def exchange_kernel(
    own_ref, table_ref, out_ref,
    own, table, spread_ref, partner, own_wide, partner_wide, field, kernel,
    partial, from_x, from_far, row_sum, from_y,
    planes_ref, copy_sem, in_send, in_recv, x_send, x_recv, y_send, y_recv, far_send, far_recv,
    opposite_sem, far_sem, go_sem,
):
    blk = lax.axis_index("blk")
    off = lax.axis_index("off")
    z, y_lo = blk // 4, blk % 4
    x, y_hi, core = off // 4, (off // 2) % 2, off % 2
    y = y_hi * 4 + y_lo

    load_own = pltpu.make_async_copy(own_ref, own, copy_sem.at[0])
    load_table = pltpu.make_async_copy(table_ref, table, copy_sem.at[1])
    load_own.start()
    load_table.start()

    def device(x, y, z, core):
        y = lax.rem(y + 8, 8)
        z = lax.rem(z + 8, 8)
        return (z * 4 + lax.rem(y, 4), (x * 2 + y // 4) * 2 + core)

    aside = jnp.where(core == 0, 0, 2 * lax.rem(y, 2) - 1)
    sign = 1 - 2 * lax.rem(z, 2)

    def dz_of(y_hi):
        even = jnp.where(core == 0, pick(x, (2, -2, 0, 4)), pick(x, (-2, 2, 4, 0)))
        odd = jnp.where(core == 0, pick(x, (3, -3, 1, -1)), pick(x, (-1, 1, -3, 3)))
        return jnp.where(y_hi == 1, even, odd * sign)

    there = lax.rem(y + aside + 8, 8)
    source = device(x, there, z + dz_of(y_hi), core)
    dz_there = dz_of(there // 4)
    target = device(x, there, jnp.where(there // 4 == 1, z - dz_there, z + dz_there), core)
    mate_y = y + 1 - 2 * lax.rem(y, 2)
    mate = device(x, mate_y, z, core)
    mate_source = device(x, mate_y - aside, z + dz_of(y_hi), core)
    target_z = lax.rem(target[0] // 4, 8)
    target_mate = device(x, there + 1 - 2 * lax.rem(there, 2), target_z, core)
    itself = (x == 2) & (y_hi == 1) & (core == 0)
    opposite = (blk, (x * 2 + 1 - y_hi) * 2 + core)

    def neighbour(ahead, other):
        cx = lax.rem(x + ahead, 4)
        return (blk, (cx * 2 + y_hi) * 2 + (1 - core if other else core))

    around = [(ahead, other) for ahead in (1, 2, 3, 0) for other in range(2) if ahead or other]

    barrier = pltpu.get_barrier_semaphore()

    def greet(device_id):
        pl.semaphore_signal(barrier, inc=1, device_id=device_id, device_id_type=MESH)

    below, above = device(x, y - 2, z, core), device(x, y + 2, z, core)
    greet(below)
    greet(above)
    for ahead, other in around:
        greet(neighbour(ahead, other))

    moves = jnp.logical_not(itself)
    early = z < EARLY
    defer_to = moves & early & (target[0] // 4 >= EARLY)
    defer_from = moves & jnp.logical_not(early) & (source[0] // 4 < EARLY)
    double_out = moves & jnp.logical_not(early) & (target_z < EARLY)
    double_in = moves & early & (source[0] // 4 >= EARLY)
    greet(mate)

    @pl.when(double_in)
    def _():
        greet(mate_source)

    @pl.when(moves & jnp.logical_not(defer_from))
    def _():
        greet(source)

    @pl.when(defer_to)
    def _():
        greet(target)

    pl.semaphore_wait(
        barrier,
        10
        + jnp.where(moves & jnp.logical_not(defer_to), 1, 0)
        + jnp.where(defer_from, 1, 0)
        + jnp.where(double_out, 1, 0),
    )

    @pl.when(defer_from)
    def _():
        pl.semaphore_signal(go_sem, inc=1, device_id=source, device_id_type=MESH)

    def arrival(k, c):
        at = pl.ds(c * CHUNK, CHUNK)
        slot = min(k, 1)
        return pltpu.make_async_remote_copy(
            src_ref=partner.at[0, at] if k == 1 else own_ref.at[at],
            dst_ref=partner.at[slot, at],
            send_sem=in_send.at[k, c],
            recv_sem=in_recv.at[slot, c],
            device_id=(target, mate, target_mate)[k],
            device_id_type=MESH,
        )

    for c in range(CHUNKS):

        @pl.when(moves & jnp.logical_not(defer_to))
        def _():
            arrival(0, c).start()

        @pl.when(double_out)
        def _():
            arrival(2, c).start()

    pl.semaphore_signal(opposite_sem, inc=1, device_id=below, device_id_type=MESH)
    fill_spread(spread_ref)
    load_own.wait()
    spread([(own, 2)], spread_ref, own_wide, 0, NG)
    fill_kernel(kernel)
    load_table.wait()

    pl.semaphore_wait(opposite_sem, 1)
    for other in range(2):
        pl.semaphore_signal(
            far_sem, inc=1, device_id=neighbour(2, other), device_id_type=MESH
        )

    @pl.when(defer_to)
    def _():
        pl.semaphore_wait(go_sem, 1)
        for c in range(CHUNKS):
            arrival(0, c).start()

    right_forward = table.at[pl.ds(0, 256)]
    right_backward = table.at[pl.ds(256, 256)]
    left_forward = table.at[pl.ds(512, NG), pl.ds(0, 3 * NG)]
    left_backward = table.at[pl.ds(512 + NG, NG), pl.ds(0, 3 * NG)]

    @pl.when(itself)
    def _():
        partner[0] = own[...]

    def pass_on(c):
        @pl.when(moves)
        def _():
            arrival(0, c).wait_recv()

        @pl.when(jnp.logical_not(double_in))
        def _():
            arrival(1, c).start()

    pass_on(0)
    for c in range(CHUNKS):
        if c + 1 < CHUNKS:
            pass_on(c + 1)
        arrival(1, c).wait_recv()
        spread([(partner.at[0], 0), (partner.at[1], 1)], spread_ref, partner_wide, c * CHUNK, CHUNK)
        at = pl.ds(c * CHUNK * NG, CHUNK * NG)
        density = own_wide[at, :] * partner_wide[at, :]
        wide = to_lanes(along_lanes(density, right_forward[...]), CHUNK)
        field[at, :] = to_rows(along_rows(wide, left_forward[...]), CHUNK)

    columns = [field[pl.ds(j, NG, stride=NG), :] for j in range(NG)]
    spectrum = along_rows(jnp.concatenate(columns, axis=1), left_forward[...])
    back = along_rows(spectrum * to_lanes(kernel[...], NG), left_backward[...])
    for j in range(NG):
        field[pl.ds(j, NG, stride=NG), :] = back[:, j * 128 : (j + 1) * 128]

    def departure(h, ahead, other):
        return pltpu.make_async_remote_copy(
            src_ref=partial.at[h, ahead, other],
            dst_ref=from_x.at[h, (4 - ahead) % 4, other],
            send_sem=x_send.at[h, ahead, other],
            recv_sem=x_recv.at[h, (4 - ahead) % 4, other],
            device_id=neighbour(ahead, other),
            device_id_type=MESH,
        )

    def straight(other):
        cx = lax.rem(x + 2, 4)
        return pltpu.make_async_remote_copy(
            src_ref=partial.at[0, 2, other],
            dst_ref=from_far.at[other],
            send_sem=far_send.at[other],
            recv_sem=far_recv.at[other],
            device_id=(blk, (cx * 2 + 1 - y_hi) * 2 + (1 - core if other else core)),
            device_id_type=MESH,
        )

    low_half = lax.broadcasted_iota(jnp.int32, (NG // 2, 128), 1) < HALF

    def slabs(h):
        kept_hi = 1 - y_hi if h == 0 else y_hi
        starts = [
            pl.multiple_of((lax.rem(x + ahead, 4) * 2 + kept_hi) * (6 * NG), 6 * NG)
            for ahead in range(4)
        ]
        spectrum = jnp.concatenate([field[pl.ds(at, 6 * NG), :] for at in starts], axis=0)
        wide = along_rows(to_lanes(spectrum, 24), left_backward[...])
        potential = along_lanes(to_rows(wide, 24), right_backward[...])
        for ahead in (1, 3, 0, 2):
            terms = (
                potential[ahead * 6 * NG : (ahead + 1) * 6 * NG]
                * partner_wide[pl.ds(starts[ahead], 6 * NG), :]
            )
            for side in range(2):
                planes = []
                for i in range(side * 3, side * 3 + 3):
                    a = terms[i * NG : i * NG + NG // 2]
                    b = terms[i * NG + NG // 2 : (i + 1) * NG]
                    swapped = pltpu.roll(jnp.where(low_half, b, a), HALF, 1)
                    planes.append(jnp.where(low_half, a, b) + swapped)
                other = jnp.where(core == side, 0, 1)
                partial[h, ahead, other] = packed(jnp.concatenate(planes, axis=0))
            for other in range(2):
                if h == 0 and ahead == 2:
                    straight(other).start()
                elif ahead or other:
                    departure(h, ahead, other).start()

    pl.semaphore_wait(far_sem, 2)
    slabs(0)
    slabs(1)

    def gathered(h):
        total = partial[h, 0, 0]
        near = [(ahead, other) for ahead, other in around if h or ahead != 2]
        for ahead, other in near:
            departure(h, ahead, other).wait()
        for ahead, other in near:
            total = total + from_x[h, ahead, other]
        return total

    row_sum[...] = gathered(0)
    last = pltpu.make_async_remote_copy(
        src_ref=row_sum,
        dst_ref=from_y,
        send_sem=y_send,
        recv_sem=y_recv,
        device_id=opposite,
        device_id_type=MESH,
    )
    last.start()
    kept = gathered(1)
    for other in range(2):
        straight(other).wait()
    kept = kept + (from_far[0] + from_far[1])

    for c in range(CHUNKS):

        @pl.when(moves)
        def _():
            arrival(0, c).wait_send()

        @pl.when(jnp.logical_not(double_in))
        def _():
            arrival(1, c).wait_send()

        @pl.when(double_out)
        def _():
            arrival(2, c).wait_send()

    last.wait()
    planes_ref[...] = unpacked(F32(-0.25) * (kept + from_y[...]))
    join_rows(planes_ref, out_ref)


def on_device(orbitals):
    anywhere = pl.BlockSpec(memory_space=pl.ANY)
    wide = pltpu.VMEM((CELLS, 128), F32)
    slab = (PACKED, 128)
    dma = pltpu.SemaphoreType.DMA
    constants = jnp.asarray(tables())
    found = pl.pallas_call(
        exchange_kernel,
        out_shape=jax.ShapeDtypeStruct((3, 1, CELLS), F32),
        in_specs=[anywhere, anywhere],
        out_specs=pl.BlockSpec(memory_space=pltpu.VMEM),
        scratch_shapes=[
            pltpu.VMEM((NG, CELLS), BF16),
            pltpu.VMEM(constants.shape, BF16),
            pltpu.VMEM((3, SPREAD, 256), BF16),
            pltpu.VMEM((2, NG, CELLS), BF16),
            wide, wide, wide, wide,
            pltpu.VMEM((2, 4, 2, *slab), F32),
            pltpu.VMEM((2, 4, 2, *slab), F32),
            pltpu.VMEM((2, *slab), F32),
            pltpu.VMEM(slab, F32),
            pltpu.VMEM(slab, F32),
            pltpu.VMEM((SLAB, 128), F32),
            dma((2,)),
            dma((3, CHUNKS)), dma((2, CHUNKS)),
            dma((2, 4, 2)), dma((2, 4, 2)),
            dma, dma,
            dma((2,)), dma((2,)),
            pltpu.SemaphoreType.REGULAR,
            pltpu.SemaphoreType.REGULAR,
            pltpu.SemaphoreType.REGULAR,
        ],
        compiler_params=pltpu.CompilerParams(
            collective_id=0, has_side_effects=True, vmem_limit_bytes=54 * 2**20 - 2**17
        ),
    )(orbitals[0], constants)
    return found.transpose(1, 0, 2)


def solution(mesh):
    return jax.shard_map(
        on_device,
        mesh=mesh,
        in_specs=(P("blk", None, None),),
        out_specs=P("blk", "off", None),
        check_vma=False,
    )
```

```python
import math

import jax
import jax.numpy as jnp
import numpy as np
from jax import lax
from jax.experimental import pallas as pl
from jax.experimental.pallas import tpu as pltpu
from jax.sharding import PartitionSpec as P

MESH = pl.DeviceIdType.MESH
F32 = jnp.float32
BF16 = jnp.bfloat16

cell_edge = 59.0
screen_rate = 0.106

NG = 48
CELLS = NG * NG
HALF = 64
SLAB = 72
PACKED = 56
EARLY = 4
CHUNKS = 3
CHUNK = NG // CHUNKS


def tables():
    n = np.arange(NG)
    basis = np.zeros((NG, NG))
    basis[0] = 1.0 / math.sqrt(NG)
    for k in range(1, NG // 2):
        basis[k] = math.sqrt(2.0 / NG) * np.cos(2.0 * math.pi * ((k * n) % NG) / NG)
        basis[NG // 2 + k] = math.sqrt(2.0 / NG) * np.sin(2.0 * math.pi * ((k * n) % NG) / NG)
    basis[NG // 2] = np.cos(math.pi * n) / math.sqrt(NG)
    high = basis.astype(jnp.bfloat16).astype(np.float64)
    low = (basis - high).astype(jnp.bfloat16).astype(np.float64)

    def right(h, l):
        table = np.zeros((256, 256))
        for p in range(2):
            at = slice(p * HALF, p * HALF + NG)
            table[at, at] = h
            table[at, 128 + p * HALF : 128 + p * HALF + NG] = l
            table[128 + p * HALF : 128 + p * HALF + NG, at] = h
        return table

    def left(h, l):
        table = np.zeros((NG, 256))
        table[:, : 3 * NG] = np.concatenate([h, h, l], axis=1)
        return table

    whole = [right(high.T, low.T), right(high, low), left(high, low), left(high.T, low.T)]
    return np.concatenate(whole, axis=0).astype(jnp.bfloat16)


def halves(v):
    high = v.astype(BF16)
    low = (v - high.astype(F32)).astype(BF16)
    return high, low


def dot(a, b):
    return jnp.dot(a, b, preferred_element_type=F32)


def along_lanes(v, table):
    high, low = halves(v)
    both = dot(jnp.concatenate([high, low], axis=1), table)
    return both[:, :128] + both[:, 128:]


def along_rows(v, table):
    high, low = halves(v)
    return dot(table, jnp.concatenate([high, low, high], axis=0))


def to_lanes(v, count):
    return jnp.concatenate([v[i * NG : (i + 1) * NG] for i in range(count)], axis=1)


def to_rows(v, count):
    return jnp.concatenate([v[:, i * 128 : (i + 1) * 128] for i in range(count)], axis=0)


WINDOWS = ((0, 128, 0), (0, 256, 96), (128, 256, 64), (256, 128, 32))
STARTS = (0, 128, 384, 640)
SPREAD = 768


def fill_spread(spread_ref):
    for (_, depth, offset), start in zip(WINDOWS, STARTS):
        row = lax.broadcasted_iota(jnp.int32, (depth, 256), 0)
        lane = lax.broadcasted_iota(jnp.int32, (depth, 256), 1)
        cell = lane % HALF
        hit = (row == offset + NG * (lane // 128) + cell) & (cell < NG)
        second = (lane // HALF) % 2 == 1
        for which, kept in enumerate((hit & ~second, hit & second, hit)):
            spread_ref[which, start : start + depth, :] = jnp.where(kept, 1.0, 0.0).astype(BF16)


def spread(parts, spread_ref, out_ref, start, count):
    for pair, (first, depth, _) in enumerate(WINDOWS):
        total = None
        for ref, which in parts:
            rows = jnp.concatenate(
                [
                    ref[start : start + count, g * 384 + first : g * 384 + first + depth]
                    for g in range(6)
                ],
                axis=0,
            )
            term = dot(rows, spread_ref[which, STARTS[pair] : STARTS[pair] + depth, :])
            total = term if total is None else total + term
        for g in range(6):
            for side in range(2):
                y = g * 8 + pair * 2 + side
                out_ref[pl.ds(start * NG + y, count, stride=NG), :] = total[
                    g * count : (g + 1) * count, side * 128 : (side + 1) * 128
                ]


def gap_lanes(rows):
    return lax.broadcasted_iota(jnp.int32, (rows, 128), 1) % HALF >= NG


def packed(slab):
    moved = [
        pltpu.roll(slab[56 + 8 * (q // 3) : 64 + 8 * (q // 3)], NG - 16 * (q % 3), 1)
        for q in range(6)
    ]
    filled = jnp.where(gap_lanes(48), jnp.concatenate(moved, axis=0), slab[:48])
    return jnp.concatenate([filled, slab[48:56]], axis=0)


def unpacked(slab):
    place = lax.broadcasted_iota(jnp.int32, (8, 128), 1) % HALF // 16
    tiles = [slab]
    for v in range(2):
        tile = jnp.zeros((8, 128), F32)
        for q in range(3):
            piece = slab[(v * 3 + q) * 8 : (v * 3 + q) * 8 + 8]
            tile = jnp.where(place == q, pltpu.roll(piece, 80 + 16 * q, 1), tile)
        tiles.append(tile)
    return jnp.concatenate(tiles, axis=0)


def signed_square(k):
    m = jnp.where(k > NG // 2, k - NG // 2, k)
    return m * m


def fill_kernel(kernel_ref):
    row = lax.broadcasted_iota(jnp.int32, (NG, 128), 0)
    lane = lax.broadcasted_iota(jnp.int32, (NG, 128), 1) % HALF
    plane = signed_square(row) + signed_square(lane)

    def one(k, carry):
        squared = plane + signed_square(k)
        wave_sq = squared.astype(F32) * F32((2.0 * math.pi / cell_edge) ** 2)
        safe_sq = jnp.where(squared == 0, F32(1.0), wave_sq)
        damped = F32(1.0) - jnp.exp(-safe_sq * F32(1.0 / (4.0 * screen_rate**2)))
        screened = F32(4.0 * math.pi) * damped / safe_sq
        value = jnp.where(squared == 0, F32(math.pi / screen_rate**2), screened)
        kernel_ref[pl.ds(pl.multiple_of(k * NG, NG), NG), :] = value
        return carry

    lax.fori_loop(0, NG, one, 0)


def join_rows(planes_ref, out_ref):
    lane = lax.broadcasted_iota(jnp.int32, (3, 128), 1)
    full = [None] * (CELLS // 128)
    for y in range(NG):
        row = planes_ref[pl.ds(y % 24, 3, stride=24), :]
        tile, at = divmod(y * NG, 128)
        row = pltpu.roll(row, (at - HALF * (y // 24)) % 128, 1)
        full[tile] = row if at == 0 else jnp.where(lane < at, full[tile], row)
        if at + NG > 128:
            full[tile + 1] = row
    for tile, row in enumerate(full):
        for plane in range(3):
            out_ref[plane, :, tile * 128 : (tile + 1) * 128] = row[plane : plane + 1]


def pick(index, values):
    result = values[-1]
    for i in range(len(values) - 1):
        result = jnp.where(index == i, values[i], result)
    return result


def exchange_kernel(
    own_ref, table_ref, out_ref,
    own, table, spread_ref, partner, own_wide, partner_wide, field, kernel,
    partial, from_x, from_far, row_sum, from_y,
    planes_ref, copy_sem, in_send, in_recv, x_send, x_recv, y_send, y_recv, far_send, far_recv,
    opposite_sem, far_sem, go_sem,
):
    blk = lax.axis_index("blk")
    off = lax.axis_index("off")
    z, y_lo = blk // 4, blk % 4
    x, y_hi, core = off // 4, (off // 2) % 2, off % 2
    y = y_hi * 4 + y_lo

    load_own = pltpu.make_async_copy(own_ref, own, copy_sem.at[0])
    load_table = pltpu.make_async_copy(table_ref, table, copy_sem.at[1])
    load_own.start()
    load_table.start()

    def device(x, y, z, core):
        y = lax.rem(y + 8, 8)
        z = lax.rem(z + 8, 8)
        return (z * 4 + lax.rem(y, 4), (x * 2 + y // 4) * 2 + core)

    aside = jnp.where(core == 0, 0, 2 * lax.rem(y, 2) - 1)
    sign = 1 - 2 * lax.rem(z, 2)

    def dz_of(y_hi):
        even = jnp.where(core == 0, pick(x, (2, -2, 0, 4)), pick(x, (-2, 2, 4, 0)))
        odd = jnp.where(core == 0, pick(x, (3, -3, 1, -1)), pick(x, (-1, 1, -3, 3)))
        return jnp.where(y_hi == 1, even, odd * sign)

    there = lax.rem(y + aside + 8, 8)
    source = device(x, there, z + dz_of(y_hi), core)
    dz_there = dz_of(there // 4)
    target = device(x, there, jnp.where(there // 4 == 1, z - dz_there, z + dz_there), core)
    mate_y = y + 1 - 2 * lax.rem(y, 2)
    mate = device(x, mate_y, z, core)
    mate_source = device(x, mate_y - aside, z + dz_of(y_hi), core)
    target_z = lax.rem(target[0] // 4, 8)
    target_mate = device(x, there + 1 - 2 * lax.rem(there, 2), target_z, core)
    itself = (x == 2) & (y_hi == 1) & (core == 0)
    opposite = (blk, (x * 2 + 1 - y_hi) * 2 + core)

    def neighbour(ahead, other):
        cx = lax.rem(x + ahead, 4)
        return (blk, (cx * 2 + y_hi) * 2 + (1 - core if other else core))

    around = [(ahead, other) for ahead in (1, 2, 3, 0) for other in range(2) if ahead or other]

    barrier = pltpu.get_barrier_semaphore()

    def greet(device_id):
        pl.semaphore_signal(barrier, inc=1, device_id=device_id, device_id_type=MESH)

    below, above = device(x, y - 2, z, core), device(x, y + 2, z, core)
    greet(below)
    greet(above)
    for ahead, other in around:
        greet(neighbour(ahead, other))

    moves = jnp.logical_not(itself)
    early = z < EARLY
    defer_to = moves & early & (target[0] // 4 >= EARLY)
    defer_from = moves & jnp.logical_not(early) & (source[0] // 4 < EARLY)
    double_out = moves & jnp.logical_not(early) & (target_z < EARLY)
    double_in = moves & early & (source[0] // 4 >= EARLY)
    greet(mate)

    @pl.when(double_in)
    def _():
        greet(mate_source)

    @pl.when(moves & jnp.logical_not(defer_from))
    def _():
        greet(source)

    @pl.when(defer_to)
    def _():
        greet(target)

    pl.semaphore_wait(
        barrier,
        10
        + jnp.where(moves & jnp.logical_not(defer_to), 1, 0)
        + jnp.where(defer_from, 1, 0)
        + jnp.where(double_out, 1, 0),
    )

    @pl.when(defer_from)
    def _():
        pl.semaphore_signal(go_sem, inc=1, device_id=source, device_id_type=MESH)

    def arrival(k, c):
        at = pl.ds(c * CHUNK, CHUNK)
        slot = min(k, 1)
        return pltpu.make_async_remote_copy(
            src_ref=partner.at[0, at] if k == 1 else own_ref.at[at],
            dst_ref=partner.at[slot, at],
            send_sem=in_send.at[k, c],
            recv_sem=in_recv.at[slot, c],
            device_id=(target, mate, target_mate)[k],
            device_id_type=MESH,
        )

    for c in range(CHUNKS):

        @pl.when(moves & jnp.logical_not(defer_to))
        def _():
            arrival(0, c).start()

        @pl.when(double_out)
        def _():
            arrival(2, c).start()

    pl.semaphore_signal(opposite_sem, inc=1, device_id=below, device_id_type=MESH)
    fill_spread(spread_ref)
    load_own.wait()
    spread([(own, 2)], spread_ref, own_wide, 0, NG)
    fill_kernel(kernel)
    load_table.wait()

    pl.semaphore_wait(opposite_sem, 1)
    for other in range(2):
        pl.semaphore_signal(
            far_sem, inc=1, device_id=neighbour(2, other), device_id_type=MESH
        )

    @pl.when(defer_to)
    def _():
        pl.semaphore_wait(go_sem, 1)
        for c in range(CHUNKS):
            arrival(0, c).start()

    right_forward = table.at[pl.ds(0, 256)]
    right_backward = table.at[pl.ds(256, 256)]
    left_forward = table.at[pl.ds(512, NG), pl.ds(0, 3 * NG)]
    left_backward = table.at[pl.ds(512 + NG, NG), pl.ds(0, 3 * NG)]

    @pl.when(itself)
    def _():
        partner[0] = own[...]

    def pass_on(c):
        @pl.when(moves)
        def _():
            arrival(0, c).wait_recv()

        @pl.when(jnp.logical_not(double_in))
        def _():
            arrival(1, c).start()

    pass_on(0)
    for c in range(CHUNKS):
        if c + 1 < CHUNKS:
            pass_on(c + 1)
        arrival(1, c).wait_recv()
        spread([(partner.at[0], 0), (partner.at[1], 1)], spread_ref, partner_wide, c * CHUNK, CHUNK)
        at = pl.ds(c * CHUNK * NG, CHUNK * NG)
        density = own_wide[at, :] * partner_wide[at, :]
        wide = to_lanes(along_lanes(density, right_forward[...]), CHUNK)
        field[at, :] = to_rows(along_rows(wide, left_forward[...]), CHUNK)

    columns = [field[pl.ds(j, NG, stride=NG), :] for j in range(NG)]
    spectrum = along_rows(jnp.concatenate(columns, axis=1), left_forward[...])
    back = along_rows(spectrum * to_lanes(kernel[...], NG), left_backward[...])
    for j in range(NG):
        field[pl.ds(j, NG, stride=NG), :] = back[:, j * 128 : (j + 1) * 128]

    def departure(h, ahead, other):
        return pltpu.make_async_remote_copy(
            src_ref=partial.at[h, ahead, other],
            dst_ref=from_x.at[h, (4 - ahead) % 4, other],
            send_sem=x_send.at[h, ahead, other],
            recv_sem=x_recv.at[h, (4 - ahead) % 4, other],
            device_id=neighbour(ahead, other),
            device_id_type=MESH,
        )

    def straight(other):
        cx = lax.rem(x + 2, 4)
        return pltpu.make_async_remote_copy(
            src_ref=partial.at[0, 2, other],
            dst_ref=from_far.at[other],
            send_sem=far_send.at[other],
            recv_sem=far_recv.at[other],
            device_id=(blk, (cx * 2 + 1 - y_hi) * 2 + (1 - core if other else core)),
            device_id_type=MESH,
        )

    low_half = lax.broadcasted_iota(jnp.int32, (NG // 2, 128), 1) < HALF

    def slabs(h):
        kept_hi = 1 - y_hi if h == 0 else y_hi
        starts = [
            pl.multiple_of((lax.rem(x + ahead, 4) * 2 + kept_hi) * (6 * NG), 6 * NG)
            for ahead in range(4)
        ]
        spectrum = jnp.concatenate([field[pl.ds(at, 6 * NG), :] for at in starts], axis=0)
        wide = along_rows(to_lanes(spectrum, 24), left_backward[...])
        potential = along_lanes(to_rows(wide, 24), right_backward[...])
        for ahead in (1, 3, 0, 2):
            terms = (
                potential[ahead * 6 * NG : (ahead + 1) * 6 * NG]
                * partner_wide[pl.ds(starts[ahead], 6 * NG), :]
            )
            for side in range(2):
                planes = []
                for i in range(side * 3, side * 3 + 3):
                    a = terms[i * NG : i * NG + NG // 2]
                    b = terms[i * NG + NG // 2 : (i + 1) * NG]
                    swapped = pltpu.roll(jnp.where(low_half, b, a), HALF, 1)
                    planes.append(jnp.where(low_half, a, b) + swapped)
                other = jnp.where(core == side, 0, 1)
                partial[h, ahead, other] = packed(jnp.concatenate(planes, axis=0))
            for other in range(2):
                if h == 0 and ahead == 2:
                    straight(other).start()
                elif ahead or other:
                    departure(h, ahead, other).start()

    pl.semaphore_wait(far_sem, 2)
    slabs(0)
    slabs(1)

    def gathered(h):
        total = partial[h, 0, 0]
        near = [(ahead, other) for ahead, other in around if h or ahead != 2]
        for ahead, other in near:
            departure(h, ahead, other).wait()
        for ahead, other in near:
            total = total + from_x[h, ahead, other]
        return total

    row_sum[...] = gathered(0)
    last = pltpu.make_async_remote_copy(
        src_ref=row_sum,
        dst_ref=from_y,
        send_sem=y_send,
        recv_sem=y_recv,
        device_id=opposite,
        device_id_type=MESH,
    )
    last.start()
    kept = gathered(1)
    for other in range(2):
        straight(other).wait()
    kept = kept + (from_far[0] + from_far[1])

    for c in range(CHUNKS):

        @pl.when(moves)
        def _():
            arrival(0, c).wait_send()

        @pl.when(jnp.logical_not(double_in))
        def _():
            arrival(1, c).wait_send()

        @pl.when(double_out)
        def _():
            arrival(2, c).wait_send()

    last.wait()
    planes_ref[...] = unpacked(F32(-0.25) * (kept + from_y[...]))
    join_rows(planes_ref, out_ref)


def on_device(orbitals):
    anywhere = pl.BlockSpec(memory_space=pl.ANY)
    wide = pltpu.VMEM((CELLS, 128), F32)
    slab = (PACKED, 128)
    dma = pltpu.SemaphoreType.DMA
    constants = jnp.asarray(tables())
    found = pl.pallas_call(
        exchange_kernel,
        out_shape=jax.ShapeDtypeStruct((3, 1, CELLS), F32),
        in_specs=[anywhere, anywhere],
        out_specs=pl.BlockSpec(memory_space=pltpu.VMEM),
        scratch_shapes=[
            pltpu.VMEM((NG, CELLS), BF16),
            pltpu.VMEM(constants.shape, BF16),
            pltpu.VMEM((3, SPREAD, 256), BF16),
            pltpu.VMEM((2, NG, CELLS), BF16),
            wide, wide, wide, wide,
            pltpu.VMEM((2, 4, 2, *slab), F32),
            pltpu.VMEM((2, 4, 2, *slab), F32),
            pltpu.VMEM((2, *slab), F32),
            pltpu.VMEM(slab, F32),
            pltpu.VMEM(slab, F32),
            pltpu.VMEM((SLAB, 128), F32),
            dma((2,)),
            dma((3, CHUNKS)), dma((2, CHUNKS)),
            dma((2, 4, 2)), dma((2, 4, 2)),
            dma, dma,
            dma((2,)), dma((2,)),
            pltpu.SemaphoreType.REGULAR,
            pltpu.SemaphoreType.REGULAR,
            pltpu.SemaphoreType.REGULAR,
        ],
        compiler_params=pltpu.CompilerParams(
            collective_id=0, has_side_effects=True, vmem_limit_bytes=54 * 2**20 - 2**17
        ),
    )(orbitals[0], constants)
    return found.transpose(1, 0, 2)


def solution(mesh):
    return jax.shard_map(
        on_device,
        mesh=mesh,
        in_specs=(P("blk", None, None),),
        out_specs=P("blk", "off", None),
        check_vma=False,
    )
```
